256 devices in a mesh: section: 8 (over x, core), expert: 32 (over z, y).
Axes of the slice: x: 4, y: 4, z: 8, core: 2. Of those that a mesh axis runs over, the one named last changes fastest.
Arguments:
- fwd_handoff: bfloat16 [8, 4096, 1536], P('section', 'expert'), may hold values from -27 to 27
- saved_input: bfloat16 [8, 4096, 1536], P('section', 'expert'), may hold values from -27 to 27
- grad_handoff: bfloat16 [8, 4096, 1536], P('section', 'expert'), may hold values from -3 to 3
- gain: float32 [8, 1536], P('section'), may hold values from 0.1 to 1.9
- route_fwd: int32 [8, 4096, 2], P('section', 'expert'), may hold values from 0 to 7, as said below
- gate_fwd: float32 [8, 4096, 2], P('section', 'expert'), may hold values from 0.1 to 1
- route_bwd: int32 [8, 4096, 2], P('section', 'expert'), may hold values from 0 to 7, as said below
- slot_bwd: int32 [8, 4096, 2], P('section', 'expert'), may hold values from 0 to 31, as said below
- gate_bwd: float32 [8, 4096, 2], P('section', 'expert'), may hold values from 0.1 to 1
- w_in: bfloat16 [8, 1536, 24576], P('section', None, 'expert'), may hold values from -0.15625 to 0.15625
- w_out: bfloat16 [8, 24576, 1536], P('section', 'expert'), may hold values from -0.109375 to 0.109375
- saved_pre: bfloat16 [8, 32768, 768], P('section', 'expert'), may hold values from -5 to 5
Outputs:
- section_out: bfloat16 [8, 4096, 1536], P('section', 'expert')
- input_grad: bfloat16 [8, 4096, 1536], P('section', 'expert')
- grad_w_in: bfloat16 [8, 1536, 24576], P('section', None, 'expert')
- grad_w_out: bfloat16 [8, 24576, 1536], P('section', 'expert')
The draws below stay inside these ranges and needn't reach their ends.
Inputs may be any that keep to these rules, and one draw needn't show every extreme that they name: `route_fwd`: each token names two different experts; in each aligned block of 128 tokens (the tokens of one device) every expert is named by exactly 32 token-choices. `route_bwd`: each token names two different experts; in each aligned block of 128 tokens (the tokens of one device) every expert is named by exactly 32 token-choices. `slot_bwd`: in each aligned block of 128 tokens, the token-choices that name one expert hold the slots 0 to 31, each once.
All inputs are finite; a program needn't handle non-finite values.
Results may differ from the reference program's by a relative error of at most 0.009.
Values may be sent and summed in bfloat16 or wider, within the bound.
No kernel may reach another device: no remote copies, remote signals or barrier semaphores. Data moves between devices by JAX's collectives and lax.ppermute only.
A program may use at most 128 MiB of HBM per device.

```python
import math
import jax
import jax.numpy as jnp
from jax import lax

D = 1536
FF = 3072
EXPERTS = 8
TOP = 2
TOK_DEV = 128
SECTIONS = 8
TOKENS = 4096
GROUP = 4
CAP = 32
N_EXPERT = 32


def scaled_field(key, field_shape):
    subkeys = jax.random.split(key, 3)
    row_total = field_shape[0] * field_shape[1]
    columns = field_shape[2]
    log_low = math.log(0.3)
    log_high = math.log(3.0)
    row_scale = jnp.exp(jax.random.uniform(subkeys[0], (row_total, 1), jnp.float32, log_low, log_high))
    col_scale = jnp.exp(jax.random.uniform(subkeys[1], (1, columns), jnp.float32, log_low, log_high))
    noise = jnp.clip(jax.random.normal(subkeys[2], (row_total, columns), jnp.float32), -3.0, 3.0)
    return (noise * row_scale * col_scale).reshape(field_shape)


def draw_fwd_handoff(key, part):
    return scaled_field(jax.random.fold_in(key, 21), (SECTIONS, TOKENS, D)).astype(jnp.bfloat16)


def draw_saved_input(key, part):
    return scaled_field(jax.random.fold_in(key, 22), (SECTIONS, TOKENS, D)).astype(jnp.bfloat16)


def route_block(key):
    rounds = TOK_DEV // EXPERTS
    subkeys = jax.random.split(key, 5)
    orders = jax.vmap(lambda single: jax.random.permutation(single, EXPERTS))(jax.random.split(subkeys[0], rounds)).astype(jnp.int32)
    step_size = jax.random.randint(subkeys[1], (rounds, 1), 1, EXPERTS).astype(jnp.int32)
    inverse = jnp.argsort(orders, axis=1).astype(jnp.int32)
    position = (inverse + step_size) % EXPERTS
    partner = jnp.take_along_axis(orders, position, axis=1)
    first_ids = jnp.broadcast_to(jnp.arange(EXPERTS, dtype=jnp.int32)[None, :], (rounds, EXPERTS))
    base_slot = jnp.broadcast_to(2 * jnp.arange(rounds, dtype=jnp.int32)[:, None], (rounds, EXPERTS))
    expert_ids = jnp.stack([first_ids, partner], axis=-1).reshape(TOK_DEV, 2)
    slot_ids = jnp.stack([base_slot, base_slot + 1], axis=-1).reshape(TOK_DEV, 2)
    relabel = jax.vmap(lambda single: jax.random.permutation(single, CAP))(jax.random.split(subkeys[2], EXPERTS)).astype(jnp.int32)
    slot_ids = relabel[expert_ids, slot_ids]
    shuffle = jax.random.permutation(subkeys[3], TOK_DEV)
    expert_ids = expert_ids[shuffle]
    slot_ids = slot_ids[shuffle]
    flipped = jax.random.randint(subkeys[4], (TOK_DEV, 1), 0, 2)
    expert_ids = jnp.where(flipped == 1, expert_ids[:, ::-1], expert_ids)
    slot_ids = jnp.where(flipped == 1, slot_ids[:, ::-1], slot_ids)
    return (expert_ids.astype(jnp.int32), slot_ids.astype(jnp.int32))


def routing(key):
    blocks = SECTIONS * TOKENS // TOK_DEV
    expert_ids, slot_ids = jax.vmap(route_block)(jax.random.split(key, blocks))
    return (expert_ids.reshape(SECTIONS, TOKENS, TOP), slot_ids.reshape(SECTIONS, TOKENS, TOP))


def draw_route_fwd(key, part):
    return routing(jax.random.fold_in(key, 31))[0]


def draw_route_bwd(key, part):
    return routing(jax.random.fold_in(key, 32))[0]


def draw_slot_bwd(key, part):
    return routing(jax.random.fold_in(key, 32))[1]


def level_of(key, shape, cuts, least, high):
    def one(dim, parts):
        steps = jax.random.uniform(jax.random.fold_in(jax.random.fold_in(key, 6), dim), (parts,), jnp.float32, least / len(cuts), high / len(cuts))
        return jnp.repeat(jnp.exp(steps), shape[dim] // parts).reshape((-1,) + (1,) * (len(shape) - dim - 1))

    level = one(*cuts[0])
    for cut in cuts[1:]:
        level = level * one(*cut)
    return level


def scatter_about(stream_key, shape, deviation, reach, pieces=(), kind=jnp.bfloat16):
    entries = jax.random.normal(stream_key, shape, jnp.float32) * deviation
    if len(pieces) > 0:
        entries = level_of(stream_key, shape, pieces, -0.22, 0.18) * entries
    return jnp.clip(entries, min=-reach, max=reach).astype(kind)


def setup_inputs(seed: int = 0) -> dict:
    key_list = jax.random.split(jax.random.key(seed), 13)
    fwd_handoff = draw_fwd_handoff(jax.random.fold_in(key_list[12], 71), 0)
    saved_input = draw_saved_input(jax.random.fold_in(key_list[12], 71), 0)
    grad_handoff = scatter_about(key_list[2], (SECTIONS, TOKENS, D), 0.5, 3.0, ((0, 8), (1, 32)))
    gain = jnp.clip(1.0 + 0.18 * jax.random.normal(key_list[3], (SECTIONS, D), jnp.float32), 0.1, 1.9)
    route_fwd = draw_route_fwd(jax.random.fold_in(key_list[12], 71), 0)
    gate_fwd = jnp.clip(0.1 + 0.9 * jax.random.uniform(key_list[5], (SECTIONS, TOKENS, TOP), jnp.float32) ** level_of(key_list[5], (SECTIONS, TOKENS, TOP), ((0, 8), (1, 32)), -0.2, 0.2), 0.1, 1.0)
    route_bwd = draw_route_bwd(jax.random.fold_in(key_list[12], 71), 0)
    slot_bwd = draw_slot_bwd(jax.random.fold_in(key_list[12], 71), 0)
    gate_bwd = jnp.clip(0.1 + 0.9 * jax.random.uniform(key_list[8], (SECTIONS, TOKENS, TOP), jnp.float32) ** level_of(key_list[8], (SECTIONS, TOKENS, TOP), ((0, 8), (1, 32)), -0.2, 0.2), 0.1, 1.0)
    w_in = scatter_about(key_list[9], (SECTIONS, D, EXPERTS * FF), D ** -0.5, 0.15625, ((0, 8), (2, 32)))
    w_out = scatter_about(key_list[10], (SECTIONS, EXPERTS * FF, D), FF ** -0.5, 0.109375, ((0, 8), (1, 32)))
    saved_pre = scatter_about(key_list[11], (SECTIONS, TOKENS * TOP * GROUP, FF // GROUP), 1.0, 5.0, ((0, 8), (1, 32)))
    return dict(fwd_handoff=fwd_handoff, saved_input=saved_input, grad_handoff=grad_handoff, gain=gain, route_fwd=route_fwd, gate_fwd=gate_fwd, route_bwd=route_bwd, slot_bwd=slot_bwd, gate_bwd=gate_bwd, w_in=w_in, w_out=w_out, saved_pre=saved_pre)


EPSILON = 1e-06
TANH_SCALE = 0.7978845608028654
CUBIC_COEF = 0.044715

def gelu_pair(pre_act):
    inner = TANH_SCALE * (pre_act + CUBIC_COEF * pre_act * pre_act * pre_act)
    tangent = jnp.tanh(inner)
    activated = 0.5 * pre_act * (1.0 + tangent)
    derivative = 0.5 * (1.0 + tangent) + 0.5 * pre_act * (1.0 - tangent * tangent) * TANH_SCALE * (1.0 + 3.0 * CUBIC_COEF * pre_act * pre_act)
    return (activated, derivative)

def normalize(row_set, gain_row):
    widened = row_set.astype(jnp.float32)
    recip = lax.rsqrt(lax.optimization_barrier(jnp.mean(widened * widened, axis=-1, keepdims=True)) + EPSILON)
    return (widened, recip, (widened * recip * gain_row).astype(jnp.bfloat16))

def slice_partials(left, right_rows):
    row_count = left.shape[0]
    hidden_size = FF // GROUP
    split_left = left.reshape(row_count, GROUP, hidden_size).astype(jnp.float32)
    split_right = right_rows.reshape(GROUP, hidden_size, D).astype(jnp.float32)
    partials = jnp.einsum('rgh,ghd->grd', split_left, split_right).astype(jnp.bfloat16)
    return lax.optimization_barrier(jnp.sum(partials.astype(jnp.float32), axis=0))

def expert_forward(row_set, w_in_part, w_out_part):
    pre_act = jnp.dot(row_set, w_in_part, preferred_element_type=jnp.float32)
    hidden = gelu_pair(pre_act)[0].astype(jnp.bfloat16)
    return slice_partials(hidden, w_out_part)

def expert_backward(row_set, grad_set, pre_act, w_in_part, w_out_part):
    activated, derivative = gelu_pair(pre_act.astype(jnp.float32))
    hidden = activated.astype(jnp.bfloat16)
    hidden_grad = jnp.dot(grad_set, w_out_part.T, preferred_element_type=jnp.float32)
    pre_grad = (hidden_grad * derivative).astype(jnp.bfloat16)
    grad_out_part = jnp.dot(hidden.T, grad_set, preferred_element_type=jnp.float32).astype(jnp.bfloat16)
    grad_in_part = jnp.dot(row_set.T, pre_grad, preferred_element_type=jnp.float32).astype(jnp.bfloat16)
    return (grad_in_part, grad_out_part, slice_partials(pre_grad, w_in_part.T))

def one_section(packed):
    arrival = packed[0]
    stash = packed[1]
    cotangent = packed[2]
    gain_row = packed[3]
    route_f = packed[4]
    gate_f = packed[5]
    route_b = packed[6]
    slot_b = packed[7]
    gate_b = packed[8]
    w_in_s = packed[9]
    w_out_s = packed[10]
    pre_s = packed[11]
    span_rows = N_EXPERT * CAP
    block_ids = jnp.arange(N_EXPERT, dtype=jnp.int32)[:, None]
    w_in_e = w_in_s.reshape(D, EXPERTS, FF).transpose(1, 0, 2)
    w_out_e = w_out_s.reshape(EXPERTS, FF, D)
    plain_fwd, recip_fwd, normed_fwd = normalize(arrival, gain_row)
    sorted_ids = jnp.argsort(route_f.reshape(N_EXPERT, TOK_DEV * TOP), axis=1).astype(jnp.int32)
    position = jnp.argsort(sorted_ids, axis=1).astype(jnp.int32)
    source_tok = (block_ids * TOK_DEV + sorted_ids // TOP).reshape(N_EXPERT, EXPERTS, CAP).transpose(1, 0, 2).reshape(-1)
    rows_fwd = normed_fwd[source_tok].reshape(EXPERTS, span_rows, D)
    expert_out = lax.map(lambda items: expert_forward(items[0], items[1], items[2]), (rows_fwd, w_in_e, w_out_e))
    target_fwd = (position // CAP * span_rows + block_ids * CAP + position % CAP).reshape(-1)
    picked = expert_out.reshape(EXPERTS * span_rows, D)[target_fwd].reshape(TOKENS, TOP, D)
    section_out = (plain_fwd + lax.optimization_barrier(jnp.sum(gate_f[:, :, None] * picked, axis=1))).astype(jnp.bfloat16)
    plain_bwd, recip_bwd, normed_bwd = normalize(stash, gain_row)
    token_block = (jnp.arange(TOKENS, dtype=jnp.int32) // TOK_DEV)[:, None]
    target_bwd = (route_b * span_rows + token_block * CAP + slot_b).reshape(-1)
    grad_choice = (gate_b[:, :, None] * cotangent.astype(jnp.float32)[:, None, :]).astype(jnp.bfloat16).reshape(TOKENS * TOP, D)
    rows_bwd = jnp.zeros((EXPERTS * span_rows, D), jnp.bfloat16).at[target_bwd].set(jnp.repeat(normed_bwd, TOP, axis=0))
    grad_rows = jnp.zeros((EXPERTS * span_rows, D), jnp.bfloat16).at[target_bwd].set(grad_choice)
    pre_e = pre_s.reshape(EXPERTS, GROUP, span_rows, FF // GROUP).transpose(0, 2, 1, 3).reshape(EXPERTS, span_rows, FF)
    grad_in_e, grad_out_e, back_rows = lax.map(lambda items: expert_backward(items[0], items[1], items[2], items[3], items[4]), (rows_bwd.reshape(EXPERTS, span_rows, D), grad_rows.reshape(EXPERTS, span_rows, D), pre_e, w_in_e, w_out_e))
    grad_w_in = grad_in_e.transpose(1, 0, 2).reshape(D, EXPERTS * FF)
    grad_w_out = grad_out_e.reshape(EXPERTS * FF, D)
    dnormed = lax.optimization_barrier(jnp.sum(back_rows.reshape(EXPERTS * span_rows, D)[target_bwd].reshape(TOKENS, TOP, D), axis=1))
    scaled = gain_row * dnormed
    cubed = recip_bwd * recip_bwd * recip_bwd
    input_grad = (cotangent.astype(jnp.float32) + recip_bwd * scaled - plain_bwd * cubed * lax.optimization_barrier(jnp.mean(scaled * plain_bwd, axis=-1, keepdims=True))).astype(jnp.bfloat16)
    return (section_out, input_grad, grad_w_in, grad_w_out)

def reference(fwd_handoff, saved_input, grad_handoff, gain, route_fwd, gate_fwd, route_bwd, slot_bwd, gate_bwd, w_in, w_out, saved_pre):
    arrival = jnp.roll(fwd_handoff, 1, axis=0)
    cotangent = jnp.roll(grad_handoff, -1, axis=0)
    results = lax.map(one_section, (arrival, saved_input, cotangent, gain, route_fwd, gate_fwd, route_bwd, slot_bwd, gate_bwd, w_in, w_out, saved_pre))
    return (results[0], results[1], results[2], results[3])
```

```python
import jax
import jax.numpy as jnp
from jax import lax
from jax.sharding import PartitionSpec as P

EXPERTS = 8


EPSILON = 1e-06
TANH_SCALE = 0.7978845608028654
CUBIC_COEF = 0.044715


def shifted(block, axis, distance):
    devices = range(lax.axis_size(axis))
    route = [((i - distance) % len(devices), i) for i in devices]
    return lax.ppermute(block, axis, route)


def gelu_pair(pre_act):
    inner = TANH_SCALE * (pre_act + CUBIC_COEF * pre_act * pre_act * pre_act)
    tangent = jnp.tanh(inner)
    activated = 0.5 * pre_act * (1.0 + tangent)
    derivative = 0.5 * (1.0 + tangent) + 0.5 * pre_act * (1.0 - tangent * tangent) * TANH_SCALE * (
        1.0 + 3.0 * CUBIC_COEF * pre_act * pre_act
    )
    return (activated, derivative)


def normalize(row_set, gain_row):
    widened = row_set.astype(jnp.float32)
    recip = lax.rsqrt(jnp.mean(widened * widened, axis=-1, keepdims=True) + EPSILON)
    return (widened, recip, (widened * recip * gain_row).astype(jnp.bfloat16))


def turned(block, groups, distance):
    route = [
        (e * groups + g, e * groups + (g + distance) % groups)
        for e in range(EXPERTS)
        for g in range(groups)
    ]
    return lax.ppermute(block, "expert", route)


def exchange(block, groups):
    index_groups = [[e * groups + g for e in range(EXPERTS)] for g in range(groups)]
    return lax.all_to_all(
        block, "expert", split_axis=0, concat_axis=0, tiled=True, axis_index_groups=index_groups
    )


def gather_group(chunk, groups):
    half = chunk.shape[0] // 2
    from_left = turned(chunk, groups, 1)
    from_right = turned(chunk, groups, -1)
    opposite_top = turned(from_left[:half], groups, 1)
    opposite_bottom = turned(from_right[half:], groups, -1)
    return [chunk, from_left, from_right, jnp.concatenate([opposite_top, opposite_bottom], axis=0)]


def add_bf16(one, other):
    return (one.astype(jnp.float32) + other.astype(jnp.float32)).astype(jnp.bfloat16)


def scatter_sum(own, to_left, to_right, to_opposite, groups):
    half = own.shape[0] // 2
    top = turned(to_opposite[:half], groups, 1)
    bottom = turned(to_opposite[half:], groups, -1)
    right_sum = jnp.concatenate([add_bf16(to_right[:half], top), to_right[half:]], axis=0)
    left_sum = jnp.concatenate([to_left[:half], add_bf16(to_left[half:], bottom)], axis=0)
    from_left = turned(right_sum, groups, 1)
    from_right = turned(left_sum, groups, -1)
    return (
        own.astype(jnp.float32) + from_left.astype(jnp.float32) + from_right.astype(jnp.float32)
    ).astype(jnp.bfloat16)


def matmul(left, right, dims):
    return lax.dot_general(left, right, (dims, ((), ())), preferred_element_type=jnp.float32)


def body(
    fwd_handoff,
    saved_input,
    grad_handoff,
    gain,
    route_fwd,
    gate_fwd,
    route_bwd,
    slot_bwd,
    gate_bwd,
    w_in,
    w_out,
    saved_pre,
):
    groups = lax.axis_size("expert") // EXPERTS
    tok_rows, features = fwd_handoff.shape[1:]
    choices = route_fwd.shape[2]
    cap_rows = tok_rows * choices // EXPERTS
    all_rows = EXPERTS * cap_rows
    mine = lax.axis_index("expert") % groups
    gain_row = gain[0]
    w_in_local = w_in[0]
    w_out_local = w_out[0]
    row_ids = jnp.arange(all_rows, dtype=jnp.int32)

    cotangent = shifted(grad_handoff, "section", -1)[0]
    arrival = shifted(fwd_handoff, "section", 1)[0]

    def send(values):
        return exchange(values.reshape(EXPERTS, cap_rows, features), groups).reshape(
            all_rows, features
        )

    target_bwd = route_bwd[0] * cap_rows + slot_bwd[0]
    hit_bwd = target_bwd[None, :, :] == row_ids[:, None, None]
    pick_bwd = jnp.any(hit_bwd, axis=2).astype(jnp.bfloat16)
    gate_pick = jnp.sum(jnp.where(hit_bwd, gate_bwd[0][None], 0.0), axis=(1, 2))
    plain_bwd, recip_bwd, normed_bwd = normalize(saved_input[0], gain_row)
    rows_bwd = matmul(pick_bwd, normed_bwd, ((1,), (0,))).astype(jnp.bfloat16)
    grad_rows = (matmul(pick_bwd, cotangent, ((1,), (0,))) * gate_pick[:, None]).astype(
        jnp.bfloat16
    )

    plain_fwd, recip_fwd, normed_fwd = normalize(arrival, gain_row)
    flat_route = route_fwd[0].reshape(-1)
    order = jnp.arange(flat_route.shape[0], dtype=jnp.int32)
    earlier = (flat_route[:, None] == flat_route[None, :]) & (order[None, :] < order[:, None])
    rank = jnp.sum(earlier.astype(jnp.int32), axis=1)
    target_fwd = (flat_route * cap_rows + rank).reshape(tok_rows, choices)
    pick_fwd = jnp.any(target_fwd[None, :, :] == row_ids[:, None, None], axis=2).astype(
        jnp.bfloat16
    )
    rows_fwd = matmul(pick_fwd, normed_fwd, ((1,), (0,))).astype(jnp.bfloat16)

    grad_chunks = gather_group(send(grad_rows), groups)
    fwd_chunks = gather_group(send(rows_fwd), groups)
    row_chunks = gather_group(send(rows_bwd), groups)

    pre_blocks = saved_pre[0].reshape(EXPERTS, groups, cap_rows, -1)
    places = [mine, (mine - 1) % groups, (mine + 1) % groups, (mine + 2) % groups]
    hidden_chunks, pre_grad_chunks, back_parts, fwd_parts = [], [], [], []
    for place, grads in zip(places, grad_chunks):
        pre = lax.dynamic_index_in_dim(pre_blocks, place, 1, keepdims=False).reshape(all_rows, -1)
        activated, derivative = gelu_pair(pre.astype(jnp.float32))
        hidden_chunks.append(activated.astype(jnp.bfloat16))
        pre_grad = (matmul(grads, w_out_local, ((1,), (1,))) * derivative).astype(jnp.bfloat16)
        pre_grad_chunks.append(pre_grad)
        back_parts.append(matmul(pre_grad, w_in_local, ((1,), (1,))).astype(jnp.bfloat16))
    for rows in fwd_chunks:
        hidden = gelu_pair(matmul(rows, w_in_local, ((1,), (0,))))[0].astype(jnp.bfloat16)
        fwd_parts.append(matmul(hidden, w_out_local, ((1,), (0,))).astype(jnp.bfloat16))

    back_sum = scatter_sum(*back_parts, groups)
    fwd_sum = scatter_sum(*fwd_parts, groups)
    return_bwd = send(back_sum)
    return_fwd = send(fwd_sum)

    pre_grads = jnp.concatenate(pre_grad_chunks, axis=0)
    grad_w_out = matmul(
        jnp.concatenate(hidden_chunks, axis=0), jnp.concatenate(grad_chunks, axis=0), ((0,), (0,))
    ).astype(jnp.bfloat16)
    grad_w_in = matmul(jnp.concatenate(row_chunks, axis=0), pre_grads, ((0,), (0,))).astype(
        jnp.bfloat16
    )

    def picked(returned, target):
        return [
            matmul(
                (target[:, k, None] == row_ids[None, :]).astype(jnp.bfloat16),
                returned,
                ((1,), (0,)),
            )
            for k in range(choices)
        ]

    section_out = plain_fwd
    for k, rows in enumerate(picked(return_fwd, target_fwd)):
        section_out = section_out + gate_fwd[0][:, k, None] * rows
    section_out = section_out.astype(jnp.bfloat16)
    dnormed = sum(picked(return_bwd, target_bwd))
    scaled = gain_row * dnormed
    cubed = recip_bwd * recip_bwd * recip_bwd
    input_grad = (
        cotangent.astype(jnp.float32)
        + recip_bwd * scaled
        - plain_bwd * cubed * jnp.mean(scaled * plain_bwd, axis=-1, keepdims=True)
    ).astype(jnp.bfloat16)
    return (section_out[None], input_grad[None], grad_w_in[None], grad_w_out[None])


def solution(mesh):
    placed = (
        P("section", "expert", None),
        P("section", "expert", None),
        P("section", "expert", None),
        P("section", None),
        P("section", "expert", None),
        P("section", "expert", None),
        P("section", "expert", None),
        P("section", "expert", None),
        P("section", "expert", None),
        P("section", None, "expert"),
        P("section", "expert", None),
        P("section", "expert", None),
    )
    return jax.shard_map(
        body,
        mesh=mesh,
        in_specs=placed,
        out_specs=(
            P("section", "expert", None),
            P("section", "expert", None),
            P("section", None, "expert"),
            P("section", "expert", None),
        ),
        check_vma=False,
    )
```

```python
import functools

import jax
import jax.numpy as jnp
from jax import lax
from jax.experimental import pallas as pl
from jax.experimental.pallas import tpu as pltpu
from jax.sharding import PartitionSpec as P

EXPERTS = 8


EPSILON = 1e-06
TANH_SCALE = 0.7978845608028654
CUBIC_COEF = 0.044715


def shifted(block, axis, distance):
    devices = range(lax.axis_size(axis))
    route = [((i - distance) % len(devices), i) for i in devices]
    return lax.ppermute(block, axis, route)


def turned(block, groups, distance):
    route = [
        (e * groups + g, e * groups + (g + distance) % groups)
        for e in range(EXPERTS)
        for g in range(groups)
    ]
    return lax.ppermute(block, "expert", route)


def exchange(block, groups):
    index_groups = [[e * groups + g for e in range(EXPERTS)] for g in range(groups)]
    return lax.all_to_all(
        block, "expert", split_axis=0, concat_axis=0, tiled=True, axis_index_groups=index_groups
    )


def gather_group(chunk, groups):
    half = chunk.shape[0] // 2
    from_left = turned(chunk, groups, 1)
    from_right = turned(chunk, groups, -1)
    opposite_top = turned(from_left[:half], groups, 1)
    opposite_bottom = turned(from_right[half:], groups, -1)
    return [chunk, from_left, from_right, opposite_top, opposite_bottom]


def after(value, *earlier):
    return lax.optimization_barrier((value, *earlier))[0]


def after(value, *earlier):
    return lax.optimization_barrier((value, *earlier))[0]


VMEM_BYTES = 30 * 1024 * 1024


def matmul(left, right, dims):
    return lax.dot_general(left, right, (dims, ((), ())), preferred_element_type=jnp.float32)


def call(kernel, out_shapes, operands, flops, in_specs=None, out_specs=None, **more):
    moved = sum(a.size * a.dtype.itemsize for a in operands)
    moved += sum(o.size * o.dtype.itemsize for o in out_shapes)
    if in_specs is None and "grid_spec" not in more:

        def whole(array):
            return pl.BlockSpec(array.shape, lambda i: (0,) * len(array.shape))

        more["grid"] = (1,)
        more["in_specs"] = [whole(a) for a in operands]
        more["out_specs"] = [whole(o) for o in out_shapes]
    elif in_specs is not None:
        more["in_specs"] = in_specs
        more["out_specs"] = out_specs
    return pl.pallas_call(
        kernel,
        out_shape=out_shapes,
        cost_estimate=pl.CostEstimate(flops=flops, bytes_accessed=moved, transcendentals=0),
        compiler_params=pltpu.CompilerParams(vmem_limit_bytes=VMEM_BYTES),
        **more,
    )(*operands)


def rms_scale(widened):
    return lax.rsqrt(jnp.mean(widened * widened, axis=-1, keepdims=True) + EPSILON)


def normed_of(tokens_ref, gain_ref):
    widened = tokens_ref[...].astype(jnp.float32)
    return (widened * rms_scale(widened) * gain_ref[...]).astype(jnp.bfloat16)


def hits_of(target, rows):
    ids = lax.broadcasted_iota(jnp.int32, (target.shape[0], rows), 1)
    return (target == ids).astype(jnp.float32).astype(jnp.bfloat16)


def forward_targets(route, cap_rows):
    tokens, choices = route.shape
    lanes = lax.broadcasted_iota(jnp.int32, (tokens, 128), 1)
    below = (
        lax.broadcasted_iota(jnp.int32, (tokens, tokens), 0)
        > lax.broadcasted_iota(jnp.int32, (tokens, tokens), 1)
    ).astype(jnp.float32)
    below = below.astype(jnp.bfloat16)
    ahead = jnp.zeros((1, 128), jnp.float32)
    targets = []
    for k in range(choices):
        expert = route[:, k : k + 1]
        named = (expert == lanes).astype(jnp.float32)
        count = matmul(below, named.astype(jnp.bfloat16), ((1,), (0,))) + ahead
        rank = jnp.sum(named * count, axis=1, keepdims=True).astype(jnp.int32)
        targets.append(expert * cap_rows + rank)
        ahead = ahead + jnp.sum(named, axis=0, keepdims=True)
    return targets


def backward_targets(route, slot, cap_rows):
    target = route * cap_rows + slot
    return [target[:, k : k + 1] for k in range(target.shape[1])]


def pick_forward_kernel(cap_rows, tokens_ref, gain_ref, route_ref, out_ref):
    normed = normed_of(tokens_ref, gain_ref)
    pick = sum(
        hits_of(t, out_ref.shape[0]).astype(jnp.float32)
        for t in forward_targets(route_ref[...], cap_rows)
    ).astype(jnp.bfloat16)
    out_ref[...] = matmul(pick, normed, ((0,), (0,))).astype(jnp.bfloat16)


def pick_backward_kernel(cap_rows, tokens_ref, gain_ref, route_ref, slot_ref, out_ref):
    normed = normed_of(tokens_ref, gain_ref)
    pick = sum(
        hits_of(t, out_ref.shape[0]).astype(jnp.float32)
        for t in backward_targets(route_ref[...], slot_ref[...], cap_rows)
    ).astype(jnp.bfloat16)
    out_ref[...] = matmul(pick, normed, ((0,), (0,))).astype(jnp.bfloat16)


def pick_grad_kernel(cap_rows, cot_ref, gate_ref, route_ref, slot_ref, out_ref):
    cot = cot_ref[...].astype(jnp.float32)
    total = None
    for k, t in enumerate(backward_targets(route_ref[...], slot_ref[...], cap_rows)):
        gated = (gate_ref[:, k : k + 1] * cot).astype(jnp.bfloat16)
        part = matmul(hits_of(t, out_ref.shape[0]), gated, ((0,), (0,)))
        total = part if total is None else total + part
    out_ref[...] = total.astype(jnp.bfloat16)


def backward_kernel(sizes, place_ref, w_in_ref, w_out_ref, *refs):
    chunks = len(sizes)
    pieces = sum(len(s) for s in sizes)
    grads = list(refs[:pieces])
    pres = refs[pieces : pieces + chunks]
    outs = refs[pieces + chunks :]
    hidden_refs = outs[:chunks]
    pre_grad_refs = outs[chunks : 2 * chunks]
    back_refs = outs[2 * chunks : 3 * chunks]
    wide = outs[3 * chunks]
    for c in range(chunks):
        row = 0
        for size in sizes[c]:
            wide[row : row + size, :] = matmul(grads.pop(0)[...], w_out_ref[...], ((1,), (1,)))
            row += size
        blocks, _, slots, _ = pres[c].shape
        for b in range(blocks):
            span = slice(b * slots, (b + 1) * slots)
            pre = pres[c][b, 0].astype(jnp.float32)
            square = pre * pre
            inner = TANH_SCALE * (pre + CUBIC_COEF * square * pre)
            tangent = jnp.tanh(inner)
            half = 0.5 * (1.0 + tangent)
            derivative = half + 0.5 * pre * (1.0 - tangent * tangent) * TANH_SCALE * (
                1.0 + 3.0 * CUBIC_COEF * square
            )
            hidden_refs[c][span, :] = (pre * half).astype(jnp.bfloat16)
            pre_grad_refs[c][span, :] = (wide[span, :] * derivative).astype(jnp.bfloat16)
        back_refs[c][...] = matmul(pre_grad_refs[c][...], w_in_ref[...], ((1,), (1,))).astype(
            jnp.bfloat16
        )


def forward_kernel(sizes, w_in_ref, w_out_ref, *refs):
    chunks = len(sizes)
    pieces = sum(len(s) for s in sizes)
    rows = list(refs[:pieces])
    outs = refs[pieces : pieces + chunks]
    wide, hidden = refs[pieces + chunks :]
    for c in range(chunks):
        row = 0
        for size in sizes[c]:
            wide[row : row + size, :] = matmul(rows.pop(0)[...], w_in_ref[...], ((1,), (0,)))
            row += size
        for b in range(row // 32):
            span = slice(b * 32, (b + 1) * 32)
            pre = wide[span, :]
            tangent = jnp.tanh(TANH_SCALE * (pre + CUBIC_COEF * pre * pre * pre))
            hidden[span, :] = (0.5 * pre * (1.0 + tangent)).astype(jnp.bfloat16)
        outs[c][...] = matmul(hidden[...], w_out_ref[...], ((1,), (0,))).astype(jnp.bfloat16)


def backward_chunks(place, grads, pre_blocks, w_in, w_out, sizes, shifts):
    experts, groups, cap_rows, hidden = pre_blocks.shape
    features = w_in.shape[0]
    rows = experts * cap_rows
    chunks = len(sizes)

    def whole(shape):
        return pl.BlockSpec(shape, lambda i, p: (0,) * len(shape))

    def shared(shift):
        return pl.BlockSpec(
            (experts, 1, cap_rows, hidden),
            lambda i, p: (0, lax.rem(p[0] + shift, groups), 0, 0),
        )

    out_shapes = (
        [jax.ShapeDtypeStruct((rows, hidden), jnp.bfloat16)] * (2 * chunks)
        + [jax.ShapeDtypeStruct((rows, features), jnp.bfloat16)] * chunks
    )
    outs = call(
        functools.partial(backward_kernel, sizes),
        out_shapes,
        [place, w_in, w_out, *grads] + [pre_blocks] * chunks,
        4 * chunks * rows * hidden * features,
        grid_spec=pltpu.PrefetchScalarGridSpec(
            num_scalar_prefetch=1,
            grid=(1,),
            in_specs=[whole(w_in.shape), whole(w_out.shape)]
            + [whole(g.shape) for g in grads]
            + [shared(s) for s in shifts],
            out_specs=[whole(o.shape) for o in out_shapes],
            scratch_shapes=[pltpu.VMEM((rows, hidden), jnp.float32)],
        ),
    )
    return outs[:chunks], outs[chunks : 2 * chunks], outs[2 * chunks :]


def forward_chunks(rows_list, w_in, w_out, sizes):
    features, hidden = w_in.shape
    rows = sum(sizes[0])
    return call(
        functools.partial(forward_kernel, sizes),
        [jax.ShapeDtypeStruct((rows, features), jnp.bfloat16)] * len(sizes),
        [w_in, w_out, *rows_list],
        4 * len(sizes) * rows * hidden * features,
        scratch_shapes=[
            pltpu.VMEM((rows, hidden), jnp.float32),
            pltpu.VMEM((rows, hidden), jnp.bfloat16),
        ],
    )


def weight_grad_kernel(lefts, rights, *refs):
    out_ref = refs[-1]

    def cut(pieces, sizes):
        spans, at = [], 0
        for ref, size in zip(pieces, sizes):
            spans.append((at, at + size, ref))
            at += size
        return spans

    left_spans = cut(refs[: len(lefts)], lefts)
    right_spans = cut(refs[len(lefts) : -1], rights)
    total = None
    for start, end, left in left_spans:
        for first, last, right in right_spans:
            low, high = max(start, first), min(end, last)
            if low >= high:
                continue
            part = matmul(
                left[low - start : high - start, :],
                right[low - first : high - first, :],
                ((0,), (0,)),
            )
            total = part if total is None else total + part
    out_ref[...] = total.astype(jnp.bfloat16)


def weight_grad(lefts, rights, tile):
    left_cols, right_cols = lefts[0].shape[1], rights[0].shape[1]
    rows = sum(a.shape[0] for a in lefts)
    return call(
        functools.partial(
            weight_grad_kernel, [a.shape[0] for a in lefts], [a.shape[0] for a in rights]
        ),
        [jax.ShapeDtypeStruct((left_cols, right_cols), jnp.bfloat16)],
        [*lefts, *rights],
        2 * rows * left_cols * right_cols,
        in_specs=[pl.BlockSpec((a.shape[0], tile), lambda i: (0, i)) for a in lefts]
        + [pl.BlockSpec(a.shape, lambda i: (0, 0)) for a in rights],
        out_specs=[pl.BlockSpec((tile, right_cols), lambda i: (i, 0))],
        grid=(left_cols // tile,),
    )[0]


def add_kernel(into_ref, more_ref, out_ref):
    out_ref[...] = (
        into_ref[...].astype(jnp.float32) + more_ref[...].astype(jnp.float32)
    ).astype(jnp.bfloat16)


def add_half(into, more, which):
    half, features = more.shape
    place = pl.BlockSpec((half, features), lambda i: (which, 0))
    return call(
        add_kernel,
        [jax.ShapeDtypeStruct(into.shape, into.dtype)],
        [into, more],
        more.size,
        in_specs=[place, pl.BlockSpec((half, features), lambda i: (0, 0))],
        out_specs=[place],
        grid=(1,),
        input_output_aliases={0: 0},
    )[0]


def sum_kernel(one_ref, two_ref, three_ref, out_ref):
    out_ref[...] = (
        one_ref[...].astype(jnp.float32)
        + two_ref[...].astype(jnp.float32)
        + three_ref[...].astype(jnp.float32)
    ).astype(jnp.bfloat16)


def sum_three(one, two, three):
    return call(
        sum_kernel, [jax.ShapeDtypeStruct(one.shape, one.dtype)], [one, two, three], 2 * one.size
    )[0]


def forward_out_kernel(cap_rows, arrival_ref, gate_ref, route_ref, returned_ref, out_ref):
    total = None
    for k, t in enumerate(forward_targets(route_ref[...], cap_rows)):
        part = gate_ref[:, k : k + 1] * matmul(
            hits_of(t, returned_ref.shape[0]), returned_ref[...], ((1,), (0,))
        )
        total = part if total is None else total + part
    out_ref[...] = (arrival_ref[...].astype(jnp.float32) + total).astype(jnp.bfloat16)


def backward_out_kernel(
    cap_rows, saved_ref, gain_ref, cot_ref, route_ref, slot_ref, returned_ref, out_ref
):
    pick = sum(
        hits_of(t, returned_ref.shape[0]).astype(jnp.float32)
        for t in backward_targets(route_ref[...], slot_ref[...], cap_rows)
    ).astype(jnp.bfloat16)
    scaled = gain_ref[...] * matmul(pick, returned_ref[...], ((1,), (0,)))
    plain = saved_ref[...].astype(jnp.float32)
    recip = rms_scale(plain)
    cubed = recip * recip * recip
    out_ref[...] = (
        cot_ref[...].astype(jnp.float32)
        + recip * scaled
        - plain * cubed * jnp.mean(scaled * plain, axis=-1, keepdims=True)
    ).astype(jnp.bfloat16)


def body(
    fwd_handoff,
    saved_input,
    grad_handoff,
    gain,
    route_fwd,
    gate_fwd,
    route_bwd,
    slot_bwd,
    gate_bwd,
    w_in,
    w_out,
    saved_pre,
):
    groups = lax.axis_size("expert") // EXPERTS
    tok_rows, features = fwd_handoff.shape[1:]
    choices = route_fwd.shape[2]
    cap_rows = tok_rows * choices // EXPERTS
    all_rows = EXPERTS * cap_rows
    half = all_rows // 2
    mine = jnp.asarray(lax.axis_index("expert") % groups, jnp.int32).reshape(1)
    w_in_local = w_in[0]
    w_out_local = w_out[0]
    pre_blocks = saved_pre[0].reshape(EXPERTS, groups, cap_rows, -1)
    rows_shape = [jax.ShapeDtypeStruct((all_rows, features), jnp.bfloat16)]
    token_shape = [jax.ShapeDtypeStruct((tok_rows, features), jnp.bfloat16)]
    pick_flops = 2 * tok_rows * all_rows * features

    def send(values):
        return exchange(values.reshape(EXPERTS, cap_rows, features), groups).reshape(
            all_rows, features
        )

    cotangent = shifted(grad_handoff, "section", -1)
    arrival = shifted(after(fwd_handoff, cotangent), "section", 1)[0]
    cotangent = cotangent[0]

    rows_bwd = call(
        functools.partial(pick_backward_kernel, cap_rows),
        rows_shape,
        [saved_input[0], gain, route_bwd[0], slot_bwd[0]],
        pick_flops,
    )[0]
    grad_rows = call(
        functools.partial(pick_grad_kernel, cap_rows),
        rows_shape,
        [cotangent, gate_bwd[0], route_bwd[0], slot_bwd[0]],
        2 * pick_flops,
    )[0]
    rows_fwd = call(
        functools.partial(pick_forward_kernel, cap_rows),
        rows_shape,
        [arrival, gain, route_fwd[0]],
        pick_flops,
    )[0]

    sent_grads = send(grad_rows)
    sent_fwd = send(after(rows_fwd, sent_grads))
    sent_rows = send(after(rows_bwd, sent_fwd))
    grads = gather_group(sent_grads, groups)
    rows = gather_group(after(sent_fwd, grads[1], grads[2]), groups)
    own_grads = after(grads[0], sent_fwd)

    def backward_of(pieces, sizes, shifts):
        return backward_chunks(
            mine, pieces, pre_blocks, w_in_local, w_out_local, sizes, shifts
        )

    whole = (all_rows,)
    halves = (half, half)
    hidden_a, pre_grad_a, back_a = backward_of(
        [own_grads, grads[1], grads[2]], [whole] * 3, (0, groups - 1, 1)
    )
    hidden_b, pre_grad_b, back_b = backward_of(
        [after(grads[3], *back_a), grads[4]], [halves], (2,)
    )
    back_opposite = back_b[0]
    back_top = turned(back_opposite[:half], groups, 1)
    back_bottom = turned(back_opposite[half:], groups, -1)

    grad_w_out = weight_grad([*hidden_a, *hidden_b], grads, 256)
    fwd_a = forward_chunks(
        [after(rows[0], grad_w_out), rows[1], rows[2]], w_in_local, w_out_local, [whole] * 3
    )
    back_left = turned(add_half(back_a[2], after(back_top, *fwd_a), 0), groups, 1)
    back_right = turned(add_half(back_a[1], back_bottom, 1), groups, -1)
    fwd_b = forward_chunks([after(rows[3], *fwd_a), rows[4]], w_in_local, w_out_local, [halves])
    fwd_opposite = fwd_b[0]
    fwd_top = turned(fwd_opposite[:half], groups, 1)
    fwd_bottom = turned(fwd_opposite[half:], groups, -1)

    back_sum = sum_three(back_a[0], back_left, back_right)
    return_bwd = send(after(back_sum, sent_rows))

    fwd_left = turned(add_half(fwd_a[2], fwd_top, 0), groups, 1)
    fwd_right = turned(add_half(fwd_a[1], fwd_bottom, 1), groups, -1)
    fwd_sum = sum_three(fwd_a[0], fwd_left, fwd_right)
    return_fwd = send(after(fwd_sum, return_bwd))
    row_chunks = gather_group(after(sent_rows, fwd_sum), groups)

    grad_w_in = weight_grad(row_chunks, [*pre_grad_a, *pre_grad_b], 256)

    section_out = call(
        functools.partial(forward_out_kernel, cap_rows),
        token_shape,
        [arrival, gate_fwd[0], route_fwd[0], return_fwd],
        2 * pick_flops,
    )[0]
    input_grad = call(
        functools.partial(backward_out_kernel, cap_rows),
        token_shape,
        [saved_input[0], gain, cotangent, route_bwd[0], slot_bwd[0], return_bwd],
        pick_flops,
    )[0]
    return (section_out[None], input_grad[None], grad_w_in[None], grad_w_out[None])


def solution(mesh):
    placed = (
        P("section", "expert", None),
        P("section", "expert", None),
        P("section", "expert", None),
        P("section", None),
        P("section", "expert", None),
        P("section", "expert", None),
        P("section", "expert", None),
        P("section", "expert", None),
        P("section", "expert", None),
        P("section", None, "expert"),
        P("section", "expert", None),
        P("section", "expert", None),
    )
    return jax.shard_map(
        body,
        mesh=mesh,
        in_specs=placed,
        out_specs=(
            P("section", "expert", None),
            P("section", "expert", None),
            P("section", None, "expert"),
            P("section", "expert", None),
        ),
        check_vma=False,
    )
```

```python
import functools

import jax
import jax.numpy as jnp
from jax import lax
from jax.experimental import pallas as pl
from jax.experimental.pallas import tpu as pltpu
from jax.sharding import PartitionSpec as P

EXPERTS = 8


EPSILON = 1e-06
TANH_SCALE = 0.7978845608028654
CUBIC_COEF = 0.044715


def shifted(block, axis, distance):
    devices = range(lax.axis_size(axis))
    route = [((i - distance) % len(devices), i) for i in devices]
    return lax.ppermute(block, axis, route)


def turned(block, groups, distance):
    route = [
        (e * groups + g, e * groups + (g + distance) % groups)
        for e in range(EXPERTS)
        for g in range(groups)
    ]
    return lax.ppermute(block, "expert", route)


def exchange(block, groups):
    index_groups = [[e * groups + g for e in range(EXPERTS)] for g in range(groups)]
    return lax.all_to_all(
        block, "expert", split_axis=0, concat_axis=0, tiled=True, axis_index_groups=index_groups
    )


def after(value, *earlier):
    return lax.optimization_barrier((value, *earlier))[0]


def after(value, *earlier):
    return lax.optimization_barrier((value, *earlier))[0]


VMEM_BYTES = 30 * 1024 * 1024


def matmul(left, right, dims):
    return lax.dot_general(left, right, (dims, ((), ())), preferred_element_type=jnp.float32)


def call(kernel, out_shapes, operands, flops, in_specs=None, out_specs=None, **more):
    moved = sum(a.size * a.dtype.itemsize for a in operands)
    moved += sum(o.size * o.dtype.itemsize for o in out_shapes)
    if in_specs is None and "grid_spec" not in more:

        def whole(array):
            return pl.BlockSpec(array.shape, lambda i: (0,) * len(array.shape))

        more["grid"] = (1,)
        more["in_specs"] = [whole(a) for a in operands]
        more["out_specs"] = [whole(o) for o in out_shapes]
    elif in_specs is not None:
        more["in_specs"] = in_specs
        more["out_specs"] = out_specs
    return pl.pallas_call(
        kernel,
        out_shape=out_shapes,
        cost_estimate=pl.CostEstimate(flops=flops, bytes_accessed=moved, transcendentals=0),
        compiler_params=pltpu.CompilerParams(vmem_limit_bytes=VMEM_BYTES),
        **more,
    )(*operands)


def rms_scale(widened):
    return lax.rsqrt(jnp.mean(widened * widened, axis=-1, keepdims=True) + EPSILON)


def normed_of(tokens_ref, gain_ref):
    widened = tokens_ref[...].astype(jnp.float32)
    return (widened * rms_scale(widened) * gain_ref[...]).astype(jnp.bfloat16)


def hits_of(target, rows):
    ids = lax.broadcasted_iota(jnp.int32, (target.shape[0], rows), 1)
    return (target == ids).astype(jnp.float32).astype(jnp.bfloat16)


def forward_targets(route, cap_rows):
    tokens, choices = route.shape
    lanes = lax.broadcasted_iota(jnp.int32, (tokens, 128), 1)
    below = (
        lax.broadcasted_iota(jnp.int32, (tokens, tokens), 0)
        > lax.broadcasted_iota(jnp.int32, (tokens, tokens), 1)
    ).astype(jnp.float32)
    below = below.astype(jnp.bfloat16)
    ahead = jnp.zeros((1, 128), jnp.float32)
    targets = []
    for k in range(choices):
        expert = route[:, k : k + 1]
        named = (expert == lanes).astype(jnp.float32)
        count = matmul(below, named.astype(jnp.bfloat16), ((1,), (0,))) + ahead
        rank = jnp.sum(named * count, axis=1, keepdims=True).astype(jnp.int32)
        targets.append(expert * cap_rows + rank)
        ahead = ahead + jnp.sum(named, axis=0, keepdims=True)
    return targets


def backward_targets(route, slot, cap_rows):
    target = route * cap_rows + slot
    return [target[:, k : k + 1] for k in range(target.shape[1])]


def pick_forward_kernel(cap_rows, tokens_ref, gain_ref, route_ref, out_ref):
    normed = normed_of(tokens_ref, gain_ref)
    pick = sum(
        hits_of(t, out_ref.shape[0]).astype(jnp.float32)
        for t in forward_targets(route_ref[...], cap_rows)
    ).astype(jnp.bfloat16)
    out_ref[...] = matmul(pick, normed, ((0,), (0,))).astype(jnp.bfloat16)


def pick_backward_kernel(cap_rows, tokens_ref, gain_ref, route_ref, slot_ref, out_ref):
    normed = normed_of(tokens_ref, gain_ref)
    pick = sum(
        hits_of(t, out_ref.shape[0]).astype(jnp.float32)
        for t in backward_targets(route_ref[...], slot_ref[...], cap_rows)
    ).astype(jnp.bfloat16)
    out_ref[...] = matmul(pick, normed, ((0,), (0,))).astype(jnp.bfloat16)


def pick_grad_kernel(cap_rows, cot_ref, gate_ref, route_ref, slot_ref, out_ref):
    cot = cot_ref[...].astype(jnp.float32)
    total = None
    for k, t in enumerate(backward_targets(route_ref[...], slot_ref[...], cap_rows)):
        gated = (gate_ref[:, k : k + 1] * cot).astype(jnp.bfloat16)
        part = matmul(hits_of(t, out_ref.shape[0]), gated, ((0,), (0,)))
        total = part if total is None else total + part
    out_ref[...] = total.astype(jnp.bfloat16)


def backward_kernel(sizes, split, place_ref, w_in_ref, w_out_ref, *refs):
    chunks = len(sizes)
    pieces = sum(len(s) for s in sizes)
    grads = list(refs[:pieces])
    pres = refs[pieces : pieces + chunks]
    outs = refs[pieces + chunks :]
    hidden_refs = outs[:chunks]
    pre_grad_refs = outs[chunks : 2 * chunks]
    back_refs = outs[2 * chunks : -1]
    wide = outs[-1]
    for c in range(chunks):
        row = 0
        for size in sizes[c]:
            wide[row : row + size, :] = matmul(grads.pop(0)[...], w_out_ref[...], ((1,), (1,)))
            row += size
        blocks, _, slots, _ = pres[c].shape
        for b in range(blocks):
            span = slice(b * slots, (b + 1) * slots)
            pre = pres[c][b, 0].astype(jnp.float32)
            square = pre * pre
            inner = TANH_SCALE * (pre + CUBIC_COEF * square * pre)
            tangent = jnp.tanh(inner)
            half = 0.5 * (1.0 + tangent)
            derivative = half + 0.5 * pre * (1.0 - tangent * tangent) * TANH_SCALE * (
                1.0 + 3.0 * CUBIC_COEF * square
            )
            hidden_refs[c][span, :] = (pre * half).astype(jnp.bfloat16)
            pre_grad_refs[c][span, :] = (wide[span, :] * derivative).astype(jnp.bfloat16)
        parts = 2 if split else 1
        for h in range(parts):
            span = slice(h * row // parts, (h + 1) * row // parts)
            back_refs[parts * c + h][...] = matmul(
                pre_grad_refs[c][span, :], w_in_ref[...], ((1,), (1,))
            ).astype(jnp.bfloat16)


def forward_kernel(sizes, split, w_in_ref, w_out_ref, *refs):
    chunks = len(sizes)
    pieces = sum(len(s) for s in sizes)
    rows = list(refs[:pieces])
    outs = refs[pieces:-2]
    wide, hidden = refs[-2:]
    for c in range(chunks):
        row = 0
        for size in sizes[c]:
            wide[row : row + size, :] = matmul(rows.pop(0)[...], w_in_ref[...], ((1,), (0,)))
            row += size
        for b in range(row // 32):
            span = slice(b * 32, (b + 1) * 32)
            pre = wide[span, :]
            tangent = jnp.tanh(TANH_SCALE * (pre + CUBIC_COEF * pre * pre * pre))
            hidden[span, :] = (0.5 * pre * (1.0 + tangent)).astype(jnp.bfloat16)
        parts = 2 if split else 1
        for h in range(parts):
            span = slice(h * row // parts, (h + 1) * row // parts)
            outs[parts * c + h][...] = matmul(
                hidden[span, :], w_out_ref[...], ((1,), (0,))
            ).astype(jnp.bfloat16)


def backward_chunks(place, grads, pre_blocks, w_in, w_out, sizes, shifts, split=False):
    experts, groups, cap_rows, hidden = pre_blocks.shape
    features = w_in.shape[0]
    rows = experts * cap_rows
    chunks = len(shifts)
    parts = 2 if split else 1

    def whole(shape):
        return pl.BlockSpec(shape, lambda i, p: (0,) * len(shape))

    def shared(shift):
        return pl.BlockSpec(
            (experts, 1, cap_rows, hidden),
            lambda i, p: (0, lax.rem(p[0] + shift, groups), 0, 0),
        )

    out_shapes = [jax.ShapeDtypeStruct((rows, hidden), jnp.bfloat16)] * (2 * chunks) + [
        jax.ShapeDtypeStruct((rows // parts, features), jnp.bfloat16)
    ] * (parts * chunks)
    outs = call(
        functools.partial(backward_kernel, sizes, split),
        out_shapes,
        [place, w_in, w_out, *grads] + [pre_blocks] * chunks,
        4 * chunks * rows * hidden * features,
        grid_spec=pltpu.PrefetchScalarGridSpec(
            num_scalar_prefetch=1,
            grid=(1,),
            in_specs=[whole(w_in.shape), whole(w_out.shape)]
            + [whole(g.shape) for g in grads]
            + [shared(s) for s in shifts],
            out_specs=[whole(o.shape) for o in out_shapes],
            scratch_shapes=[pltpu.VMEM((rows, hidden), jnp.float32)],
        ),
    )
    return outs[:chunks], outs[chunks : 2 * chunks], outs[2 * chunks :]


def forward_chunks(rows_list, w_in, w_out, sizes, split=False):
    features, hidden = w_in.shape
    rows = sum(sizes[0])
    parts = 2 if split else 1
    return call(
        functools.partial(forward_kernel, sizes, split),
        [jax.ShapeDtypeStruct((rows // parts, features), jnp.bfloat16)] * (parts * len(sizes)),
        [w_in, w_out, *rows_list],
        4 * len(sizes) * rows * hidden * features,
        scratch_shapes=[
            pltpu.VMEM((rows, hidden), jnp.float32),
            pltpu.VMEM((rows, hidden), jnp.bfloat16),
        ],
    )


def weight_grad_kernel(lefts, rights, *refs):
    out_ref = refs[-1]

    def cut(pieces, sizes):
        spans, at = [], 0
        for ref, size in zip(pieces, sizes):
            spans.append((at, at + size, ref))
            at += size
        return spans

    left_spans = cut(refs[: len(lefts)], lefts)
    right_spans = cut(refs[len(lefts) : -1], rights)
    total = None
    for start, end, left in left_spans:
        for first, last, right in right_spans:
            low, high = max(start, first), min(end, last)
            if low >= high:
                continue
            part = matmul(
                left[low - start : high - start, :],
                right[low - first : high - first, :],
                ((0,), (0,)),
            )
            total = part if total is None else total + part
    out_ref[...] = total.astype(jnp.bfloat16)


def weight_grad(lefts, rights, tile):
    left_cols, right_cols = lefts[0].shape[1], rights[0].shape[1]
    rows = sum(a.shape[0] for a in lefts)
    return call(
        functools.partial(
            weight_grad_kernel, [a.shape[0] for a in lefts], [a.shape[0] for a in rights]
        ),
        [jax.ShapeDtypeStruct((left_cols, right_cols), jnp.bfloat16)],
        [*lefts, *rights],
        2 * rows * left_cols * right_cols,
        in_specs=[pl.BlockSpec((a.shape[0], tile), lambda i: (0, i)) for a in lefts]
        + [pl.BlockSpec(a.shape, lambda i: (0, 0)) for a in rights],
        out_specs=[pl.BlockSpec((tile, right_cols), lambda i: (i, 0))],
        grid=(left_cols // tile,),
    )[0]


def exchanged_grad_kernel(rows_ref, *refs):
    out_ref = refs[-1]
    blocks, chunks, slots, tile = rows_ref.shape
    total = None
    for c in range(chunks):
        rows = rows_ref[:, c].reshape(blocks * slots, tile)
        part = matmul(rows, refs[c][...], ((0,), (0,)))
        total = part if total is None else total + part
    out_ref[...] = total.astype(jnp.bfloat16)


def exchanged_grad(rows, rights, tile):
    blocks, chunks, slots, features = rows.shape
    hidden = rights[0].shape[1]
    return call(
        exchanged_grad_kernel,
        [jax.ShapeDtypeStruct((features, hidden), jnp.bfloat16)],
        [rows, *rights],
        2 * blocks * chunks * slots * features * hidden,
        in_specs=[pl.BlockSpec((blocks, chunks, slots, tile), lambda i: (0, 0, 0, i))]
        + [pl.BlockSpec(a.shape, lambda i: (0, 0)) for a in rights],
        out_specs=[pl.BlockSpec((tile, hidden), lambda i: (i, 0))],
        grid=(features // tile,),
    )[0]


def assemble_kernel(own_ref, left_ref, right_ref, top_ref, bottom_ref, out_ref, sems):
    upper = top_ref.shape[0]
    copies = [
        (own_ref, out_ref.at[:, 0]),
        (left_ref, out_ref.at[:, 1]),
        (right_ref, out_ref.at[:, 2]),
        (top_ref, out_ref.at[:upper, 3]),
        (bottom_ref, out_ref.at[upper:, 3]),
    ]
    started = [
        pltpu.make_async_copy(source, target, sems.at[n])
        for n, (source, target) in enumerate(copies)
    ]
    for copy in started:
        copy.start()
    for copy in started:
        copy.wait()


def assemble(pieces, cap_rows):
    features = pieces[0].shape[1]
    shaped = [p.reshape(-1, cap_rows, features) for p in pieces]
    experts = shaped[0].shape[0]
    anywhere = pl.BlockSpec(memory_space=pl.ANY)
    return call(
        assemble_kernel,
        [jax.ShapeDtypeStruct((experts, 4, cap_rows, features), jnp.bfloat16)],
        shaped,
        0,
        in_specs=[anywhere] * 5,
        out_specs=[pl.BlockSpec(memory_space=pltpu.HBM)],
        scratch_shapes=[pltpu.SemaphoreType.DMA((5,))],
    )[0]


def add_kernel(into_ref, more_ref, out_ref):
    out_ref[...] = (
        into_ref[...].astype(jnp.float32) + more_ref[...].astype(jnp.float32)
    ).astype(jnp.bfloat16)


def add_half(into, more, which):
    half, features = more.shape
    place = pl.BlockSpec((half, features), lambda i: (which, 0))
    return call(
        add_kernel,
        [jax.ShapeDtypeStruct(into.shape, into.dtype)],
        [into, more],
        more.size,
        in_specs=[place, pl.BlockSpec((half, features), lambda i: (0, 0))],
        out_specs=[place],
        grid=(1,),
        input_output_aliases={0: 0},
    )[0]


def sum_kernel(one_ref, two_ref, three_ref, out_ref):
    out_ref[...] = (
        one_ref[...].astype(jnp.float32)
        + two_ref[...].astype(jnp.float32)
        + three_ref[...].astype(jnp.float32)
    ).astype(jnp.bfloat16)


def sum_three(one, two, three):
    return call(
        sum_kernel, [jax.ShapeDtypeStruct(one.shape, one.dtype)], [one, two, three], 2 * one.size
    )[0]


def forward_out_kernel(cap_rows, arrival_ref, gate_ref, route_ref, returned_ref, out_ref):
    total = None
    for k, t in enumerate(forward_targets(route_ref[...], cap_rows)):
        part = gate_ref[:, k : k + 1] * matmul(
            hits_of(t, returned_ref.shape[0]), returned_ref[...], ((1,), (0,))
        )
        total = part if total is None else total + part
    out_ref[...] = (arrival_ref[...].astype(jnp.float32) + total).astype(jnp.bfloat16)


def backward_out_kernel(
    cap_rows, saved_ref, gain_ref, cot_ref, route_ref, slot_ref, returned_ref, out_ref
):
    pick = sum(
        hits_of(t, returned_ref.shape[0]).astype(jnp.float32)
        for t in backward_targets(route_ref[...], slot_ref[...], cap_rows)
    ).astype(jnp.bfloat16)
    scaled = gain_ref[...] * matmul(pick, returned_ref[...], ((1,), (0,)))
    plain = saved_ref[...].astype(jnp.float32)
    recip = rms_scale(plain)
    cubed = recip * recip * recip
    out_ref[...] = (
        cot_ref[...].astype(jnp.float32)
        + recip * scaled
        - plain * cubed * jnp.mean(scaled * plain, axis=-1, keepdims=True)
    ).astype(jnp.bfloat16)


def body(
    fwd_handoff,
    saved_input,
    grad_handoff,
    gain,
    route_fwd,
    gate_fwd,
    route_bwd,
    slot_bwd,
    gate_bwd,
    w_in,
    w_out,
    saved_pre,
):
    groups = lax.axis_size("expert") // EXPERTS
    tok_rows, features = fwd_handoff.shape[1:]
    choices = route_fwd.shape[2]
    cap_rows = tok_rows * choices // EXPERTS
    all_rows = EXPERTS * cap_rows
    half = all_rows // 2
    mine = jnp.asarray(lax.axis_index("expert") % groups, jnp.int32).reshape(1)
    w_in_local = w_in[0]
    w_out_local = w_out[0]
    pre_blocks = saved_pre[0].reshape(EXPERTS, groups, cap_rows, -1)
    rows_shape = [jax.ShapeDtypeStruct((all_rows, features), jnp.bfloat16)]
    token_shape = [jax.ShapeDtypeStruct((tok_rows, features), jnp.bfloat16)]
    pick_flops = 2 * tok_rows * all_rows * features

    def send(values):
        return exchange(values.reshape(EXPERTS, -1, features), groups).reshape(-1, features)

    def halves_of(chunk):
        return chunk[:half], chunk[half:]

    cotangent = shifted(grad_handoff, "section", -1)
    arrival = shifted(after(fwd_handoff, cotangent), "section", 1)[0]
    cotangent = cotangent[0]

    rows_bwd = call(
        functools.partial(pick_backward_kernel, cap_rows),
        rows_shape,
        [saved_input[0], gain, route_bwd[0], slot_bwd[0]],
        pick_flops,
    )[0]
    rows_left, rows_right = turned(rows_bwd, groups, 1), turned(rows_bwd, groups, -1)
    rows_left_top, rows_right_bottom = rows_left[:half], rows_right[half:]
    rows_top = turned(rows_left_top, groups, 1)
    rows_bottom = turned(rows_right_bottom, groups, -1)

    grad_rows = call(
        functools.partial(pick_grad_kernel, cap_rows),
        rows_shape,
        [after(cotangent, rows_bwd), gate_bwd[0], route_bwd[0], slot_bwd[0]],
        2 * pick_flops,
    )[0]
    rows_fwd = call(
        functools.partial(pick_forward_kernel, cap_rows),
        rows_shape,
        [after(arrival, rows_left_top, rows_right_bottom), gain, route_fwd[0]],
        pick_flops,
    )[0]

    grads = send(grad_rows)
    grads_left, grads_right = turned(grads, groups, 1), turned(grads, groups, -1)
    sent_fwd = send(after(rows_fwd, grads))
    whole, halves = (all_rows,), (half, half)
    hidden_0, pre_grad_0, back_0 = backward_chunks(
        mine, [after(grads, rows_top, rows_bottom)], pre_blocks, w_in_local, w_out_local, [whole], (0,)
    )
    grads_left_top, grads_right_bottom = grads_left[:half], grads_right[half:]
    grads_top = turned(grads_left_top, groups, 1)
    grads_bottom = turned(grads_right_bottom, groups, -1)
    assembled = assemble(
        [after(rows_bwd, grads_left_top, grads_right_bottom, *back_0), rows_left, rows_right, rows_top, rows_bottom], cap_rows
    )
    ready = after(sent_fwd, grads_left, grads_right)
    left, right = turned(ready, groups, 1), turned(ready, groups, -1)
    sent_rows = send(after(assembled, sent_fwd))

    hidden_1, pre_grad_1, back_1 = backward_chunks(
        mine,
        [after(grads_left, sent_fwd), grads_right],
        pre_blocks,
        w_in_local,
        w_out_local,
        [whole] * 2,
        (groups - 1, 1),
    )
    hidden_2, pre_grad_2, back_2 = backward_chunks(
        mine,
        [after(grads_top, *back_1), grads_bottom],
        pre_blocks,
        w_in_local,
        w_out_local,
        [halves],
        (2,),
        split=True,
    )
    back_top = turned(back_2[0], groups, 1)
    back_bottom = turned(back_2[1], groups, -1)

    left_top, right_bottom = left[:half], right[half:]
    opposite_top = turned(left_top, groups, 1)
    opposite_bottom = turned(right_bottom, groups, -1)
    grad_w_out = weight_grad(
        [*hidden_0, *hidden_1, *hidden_2],
        [after(grads, left_top, right_bottom), grads_left, grads_right, grads_top, grads_bottom],
        256,
    )
    fwd_0 = forward_chunks([after(sent_fwd, left_top, right_bottom)], w_in_local, w_out_local, [whole])

    arrived = (grad_w_out, *fwd_0, opposite_top, opposite_bottom)
    back_to_left = add_half(back_1[1], after(back_top, *arrived), 0)
    back_to_right = add_half(back_1[0], after(back_bottom, *arrived), 1)
    back_left = turned(back_to_left, groups, 1)
    back_right = turned(back_to_right, groups, -1)
    fwd_1 = forward_chunks(
        [after(left, back_to_left, back_to_right), right], w_in_local, w_out_local, [whole] * 2
    )
    fwd_2 = forward_chunks(
        [after(opposite_top, *fwd_1), opposite_bottom], w_in_local, w_out_local, [halves], split=True
    )
    fwd_top = turned(fwd_2[0], groups, 1)
    fwd_bottom = turned(fwd_2[1], groups, -1)

    back_sum = sum_three(after(back_0[0], *fwd_2), back_left, back_right)
    fwd_to_left = add_half(fwd_1[1], fwd_top, 0)
    fwd_to_right = add_half(fwd_1[0], fwd_bottom, 1)
    return_bwd = send(after(back_sum, sent_rows, fwd_to_left, fwd_to_right))
    grad_w_in = exchanged_grad(
        sent_rows.reshape(assembled.shape), [*pre_grad_0, *pre_grad_1, *pre_grad_2], 256
    )

    fwd_left = turned(fwd_to_left, groups, 1)
    fwd_right = turned(fwd_to_right, groups, -1)
    fwd_sum = sum_three(fwd_0[0], after(fwd_left, grad_w_in), fwd_right)
    return_fwd = send(after(fwd_sum, return_bwd))

    section_out = call(
        functools.partial(forward_out_kernel, cap_rows),
        token_shape,
        [arrival, gate_fwd[0], route_fwd[0], return_fwd],
        2 * pick_flops,
    )[0]
    input_grad = call(
        functools.partial(backward_out_kernel, cap_rows),
        token_shape,
        [saved_input[0], gain, cotangent, route_bwd[0], slot_bwd[0], return_bwd],
        pick_flops,
    )[0]
    return (section_out[None], input_grad[None], grad_w_in[None], grad_w_out[None])


def solution(mesh):
    placed = (
        P("section", "expert", None),
        P("section", "expert", None),
        P("section", "expert", None),
        P("section", None),
        P("section", "expert", None),
        P("section", "expert", None),
        P("section", "expert", None),
        P("section", "expert", None),
        P("section", "expert", None),
        P("section", None, "expert"),
        P("section", "expert", None),
        P("section", "expert", None),
    )
    return jax.shard_map(
        body,
        mesh=mesh,
        in_specs=placed,
        out_specs=(
            P("section", "expert", None),
            P("section", "expert", None),
            P("section", None, "expert"),
            P("section", "expert", None),
        ),
        check_vma=False,
    )
```

```python
import functools

import jax
import jax.numpy as jnp
from jax import lax
from jax.experimental import pallas as pl
from jax.experimental.pallas import tpu as pltpu
from jax.sharding import PartitionSpec as P

EXPERTS = 8


EPSILON = 1e-06
TANH_SCALE = 0.7978845608028654
CUBIC_COEF = 0.044715


def shifted(block, axis, distance):
    devices = range(lax.axis_size(axis))
    route = [((i - distance) % len(devices), i) for i in devices]
    return lax.ppermute(block, axis, route)


def turned(block, groups, distance):
    route = [
        (e * groups + g, e * groups + (g + distance) % groups)
        for e in range(EXPERTS)
        for g in range(groups)
    ]
    return lax.ppermute(block, "expert", route)


def exchange(block, groups):
    index_groups = [[e * groups + g for e in range(EXPERTS)] for g in range(groups)]
    return lax.all_to_all(
        block, "expert", split_axis=0, concat_axis=0, tiled=True, axis_index_groups=index_groups
    )


def after(value, *earlier):
    return lax.optimization_barrier((value, *earlier))[0]


def after(value, *earlier):
    return lax.optimization_barrier((value, *earlier))[0]


VMEM_BYTES = 30 * 1024 * 1024


def matmul(left, right, dims):
    return lax.dot_general(left, right, (dims, ((), ())), preferred_element_type=jnp.float32)


def call(kernel, out_shapes, operands, flops, in_specs=None, out_specs=None, **more):
    moved = sum(a.size * a.dtype.itemsize for a in operands)
    moved += sum(o.size * o.dtype.itemsize for o in out_shapes)
    if in_specs is None and "grid_spec" not in more:

        def whole(array):
            return pl.BlockSpec(array.shape, lambda i: (0,) * len(array.shape))

        more["grid"] = (1,)
        more["in_specs"] = [whole(a) for a in operands]
        more["out_specs"] = [whole(o) for o in out_shapes]
    elif in_specs is not None:
        more["in_specs"] = in_specs
        more["out_specs"] = out_specs
    return pl.pallas_call(
        kernel,
        out_shape=out_shapes,
        cost_estimate=pl.CostEstimate(flops=flops, bytes_accessed=moved, transcendentals=0),
        compiler_params=pltpu.CompilerParams(vmem_limit_bytes=VMEM_BYTES),
        **more,
    )(*operands)


def rms_scale(widened):
    return lax.rsqrt(jnp.mean(widened * widened, axis=-1, keepdims=True) + EPSILON)


def normed_of(tokens_ref, gain_ref):
    widened = tokens_ref[...].astype(jnp.float32)
    return (widened * rms_scale(widened) * gain_ref[...]).astype(jnp.bfloat16)


def hits_of(target, rows):
    ids = lax.broadcasted_iota(jnp.int32, (target.shape[0], rows), 1)
    return (target == ids).astype(jnp.float32).astype(jnp.bfloat16)


def forward_targets(route, cap_rows):
    tokens, choices = route.shape
    lanes = lax.broadcasted_iota(jnp.int32, (tokens, 128), 1)
    below = (
        lax.broadcasted_iota(jnp.int32, (tokens, tokens), 0)
        > lax.broadcasted_iota(jnp.int32, (tokens, tokens), 1)
    ).astype(jnp.float32)
    below = below.astype(jnp.bfloat16)
    ahead = jnp.zeros((1, 128), jnp.float32)
    targets = []
    for k in range(choices):
        expert = route[:, k : k + 1]
        named = (expert == lanes).astype(jnp.float32)
        count = matmul(below, named.astype(jnp.bfloat16), ((1,), (0,))) + ahead
        rank = jnp.sum(named * count, axis=1, keepdims=True).astype(jnp.int32)
        targets.append(expert * cap_rows + rank)
        ahead = ahead + jnp.sum(named, axis=0, keepdims=True)
    return targets


def backward_targets(route, slot, cap_rows):
    target = route * cap_rows + slot
    return [target[:, k : k + 1] for k in range(target.shape[1])]


def pick_forward_kernel(cap_rows, tokens_ref, gain_ref, route_ref, out_ref):
    normed = normed_of(tokens_ref, gain_ref)
    pick = sum(
        hits_of(t, out_ref.shape[0]).astype(jnp.float32)
        for t in forward_targets(route_ref[...], cap_rows)
    ).astype(jnp.bfloat16)
    out_ref[...] = matmul(pick, normed, ((0,), (0,))).astype(jnp.bfloat16)


def tagged_kernel(tokens_ref, gain_ref, route_ref, slot_ref, out_ref):
    tokens, features = tokens_ref.shape
    choices = route_ref.shape[1]
    out_ref[:, :features] = normed_of(tokens_ref, gain_ref)
    lanes = lax.broadcasted_iota(jnp.int32, (tokens, out_ref.shape[1] - features), 1)
    tags = jnp.zeros(lanes.shape, jnp.int32)
    for k in range(choices):
        tags = jnp.where(lanes == k, route_ref[:, k : k + 1], tags)
        tags = jnp.where(lanes == choices + k, slot_ref[:, k : k + 1], tags)
    out_ref[:, features:] = tags.astype(jnp.float32).astype(jnp.bfloat16)


def picked_rows_kernel(choices, own_ref, left_ref, right_ref, top_ref, bottom_ref, out_ref):
    experts, _, cap_rows, features = out_ref.shape
    for c, pieces in enumerate(((own_ref,), (left_ref,), (right_ref,), (top_ref, bottom_ref))):
        rows = None
        for ref in pieces:
            tags = ref[:, features:].astype(jnp.float32).astype(jnp.int32)
            pick = None
            for k in range(choices):
                target = tags[:, k : k + 1] * cap_rows + tags[:, choices + k : choices + k + 1]
                hit = hits_of(target, experts * cap_rows).astype(jnp.float32)
                pick = hit if pick is None else pick + hit
            part = matmul(pick.astype(jnp.bfloat16), ref[:, :features], ((0,), (0,)))
            rows = part if rows is None else rows + part
        out_ref[:, c] = rows.astype(jnp.bfloat16).reshape(experts, cap_rows, features)


def cut_kernel(left_ref, right_ref, top_ref, bottom_ref, sems):
    half = top_ref.shape[0]
    copies = [
        pltpu.make_async_copy(left_ref.at[:half], top_ref, sems.at[0]),
        pltpu.make_async_copy(right_ref.at[half:], bottom_ref, sems.at[1]),
    ]
    for copy in copies:
        copy.start()
    for copy in copies:
        copy.wait()


def cut_halves(left, right):
    anywhere = pl.BlockSpec(memory_space=pl.ANY)
    return call(
        cut_kernel,
        [jax.ShapeDtypeStruct((left.shape[0] // 2, left.shape[1]), left.dtype)] * 2,
        [left, right],
        0,
        in_specs=[anywhere] * 2,
        out_specs=[anywhere] * 2,
        scratch_shapes=[pltpu.SemaphoreType.DMA((2,))],
    )


def pick_grad_kernel(cap_rows, cot_ref, gate_ref, route_ref, slot_ref, out_ref):
    cot = cot_ref[...].astype(jnp.float32)
    total = None
    for k, t in enumerate(backward_targets(route_ref[...], slot_ref[...], cap_rows)):
        gated = (gate_ref[:, k : k + 1] * cot).astype(jnp.bfloat16)
        part = matmul(hits_of(t, out_ref.shape[0]), gated, ((0,), (0,)))
        total = part if total is None else total + part
    out_ref[...] = total.astype(jnp.bfloat16)


def backward_kernel(sizes, split, place_ref, w_in_ref, w_out_ref, *refs):
    chunks = len(sizes)
    pieces = sum(len(s) for s in sizes)
    grads = list(refs[:pieces])
    pres = refs[pieces : pieces + chunks]
    outs = refs[pieces + chunks :]
    hidden_refs = outs[:chunks]
    pre_grad_refs = outs[chunks : 2 * chunks]
    back_refs = outs[2 * chunks : -1]
    wide = outs[-1]
    for c in range(chunks):
        row = 0
        for size in sizes[c]:
            wide[row : row + size, :] = matmul(grads.pop(0)[...], w_out_ref[...], ((1,), (1,)))
            row += size
        blocks, _, slots, _ = pres[c].shape
        for b in range(blocks):
            span = slice(b * slots, (b + 1) * slots)
            pre = pres[c][b, 0].astype(jnp.float32)
            square = pre * pre
            inner = TANH_SCALE * (pre + CUBIC_COEF * square * pre)
            tangent = jnp.tanh(inner)
            half = 0.5 * (1.0 + tangent)
            derivative = half + 0.5 * pre * (1.0 - tangent * tangent) * TANH_SCALE * (
                1.0 + 3.0 * CUBIC_COEF * square
            )
            hidden_refs[c][span, :] = (pre * half).astype(jnp.bfloat16)
            pre_grad_refs[c][span, :] = (wide[span, :] * derivative).astype(jnp.bfloat16)
        parts = 2 if split else 1
        for h in range(parts):
            span = slice(h * row // parts, (h + 1) * row // parts)
            back_refs[parts * c + h][...] = matmul(
                pre_grad_refs[c][span, :], w_in_ref[...], ((1,), (1,))
            ).astype(jnp.bfloat16)


def forward_kernel(sizes, split, w_in_ref, w_out_ref, *refs):
    chunks = len(sizes)
    pieces = sum(len(s) for s in sizes)
    rows = list(refs[:pieces])
    outs = refs[pieces:-2]
    wide, hidden = refs[-2:]
    for c in range(chunks):
        row = 0
        for size in sizes[c]:
            wide[row : row + size, :] = matmul(rows.pop(0)[...], w_in_ref[...], ((1,), (0,)))
            row += size
        for b in range(row // 32):
            span = slice(b * 32, (b + 1) * 32)
            pre = wide[span, :]
            tangent = jnp.tanh(TANH_SCALE * (pre + CUBIC_COEF * pre * pre * pre))
            hidden[span, :] = (0.5 * pre * (1.0 + tangent)).astype(jnp.bfloat16)
        parts = 2 if split else 1
        for h in range(parts):
            span = slice(h * row // parts, (h + 1) * row // parts)
            outs[parts * c + h][...] = matmul(
                hidden[span, :], w_out_ref[...], ((1,), (0,))
            ).astype(jnp.bfloat16)


def backward_chunks(place, grads, pre_blocks, w_in, w_out, sizes, shifts, split=False):
    experts, groups, cap_rows, hidden = pre_blocks.shape
    features = w_in.shape[0]
    rows = experts * cap_rows
    chunks = len(shifts)
    parts = 2 if split else 1

    def whole(shape):
        return pl.BlockSpec(shape, lambda i, p: (0,) * len(shape))

    def shared(shift):
        return pl.BlockSpec(
            (experts, 1, cap_rows, hidden),
            lambda i, p: (0, lax.rem(p[0] + shift, groups), 0, 0),
        )

    out_shapes = [jax.ShapeDtypeStruct((rows, hidden), jnp.bfloat16)] * (2 * chunks) + [
        jax.ShapeDtypeStruct((rows // parts, features), jnp.bfloat16)
    ] * (parts * chunks)
    outs = call(
        functools.partial(backward_kernel, sizes, split),
        out_shapes,
        [place, w_in, w_out, *grads] + [pre_blocks] * chunks,
        4 * chunks * rows * hidden * features,
        grid_spec=pltpu.PrefetchScalarGridSpec(
            num_scalar_prefetch=1,
            grid=(1,),
            in_specs=[whole(w_in.shape), whole(w_out.shape)]
            + [whole(g.shape) for g in grads]
            + [shared(s) for s in shifts],
            out_specs=[whole(o.shape) for o in out_shapes],
            scratch_shapes=[pltpu.VMEM((rows, hidden), jnp.float32)],
        ),
    )
    return outs[:chunks], outs[chunks : 2 * chunks], outs[2 * chunks :]


def forward_chunks(rows_list, w_in, w_out, sizes, split=False):
    features, hidden = w_in.shape
    rows = sum(sizes[0])
    parts = 2 if split else 1
    return call(
        functools.partial(forward_kernel, sizes, split),
        [jax.ShapeDtypeStruct((rows // parts, features), jnp.bfloat16)] * (parts * len(sizes)),
        [w_in, w_out, *rows_list],
        4 * len(sizes) * rows * hidden * features,
        scratch_shapes=[
            pltpu.VMEM((rows, hidden), jnp.float32),
            pltpu.VMEM((rows, hidden), jnp.bfloat16),
        ],
    )


def weight_grad_kernel(lefts, rights, *refs):
    out_ref = refs[-1]

    def cut(pieces, sizes):
        spans, at = [], 0
        for ref, size in zip(pieces, sizes):
            spans.append((at, at + size, ref))
            at += size
        return spans

    left_spans = cut(refs[: len(lefts)], lefts)
    right_spans = cut(refs[len(lefts) : -1], rights)
    total = None
    for start, end, left in left_spans:
        for first, last, right in right_spans:
            low, high = max(start, first), min(end, last)
            if low >= high:
                continue
            part = matmul(
                left[low - start : high - start, :],
                right[low - first : high - first, :],
                ((0,), (0,)),
            )
            total = part if total is None else total + part
    out_ref[...] = total.astype(jnp.bfloat16)


def weight_grad(lefts, rights, tile):
    left_cols, right_cols = lefts[0].shape[1], rights[0].shape[1]
    rows = sum(a.shape[0] for a in lefts)
    return call(
        functools.partial(
            weight_grad_kernel, [a.shape[0] for a in lefts], [a.shape[0] for a in rights]
        ),
        [jax.ShapeDtypeStruct((left_cols, right_cols), jnp.bfloat16)],
        [*lefts, *rights],
        2 * rows * left_cols * right_cols,
        in_specs=[pl.BlockSpec((a.shape[0], tile), lambda i: (0, i)) for a in lefts]
        + [pl.BlockSpec(a.shape, lambda i: (0, 0)) for a in rights],
        out_specs=[pl.BlockSpec((tile, right_cols), lambda i: (i, 0))],
        grid=(left_cols // tile,),
    )[0]


def exchanged_grad_kernel(rows_ref, *refs):
    out_ref = refs[-1]
    blocks, chunks, slots, tile = rows_ref.shape
    total = None
    for c in range(chunks):
        rows = rows_ref[:, c].reshape(blocks * slots, tile)
        part = matmul(rows, refs[c][...], ((0,), (0,)))
        total = part if total is None else total + part
    out_ref[...] = total.astype(jnp.bfloat16)


def exchanged_grad(rows, rights, tile):
    blocks, chunks, slots, features = rows.shape
    hidden = rights[0].shape[1]
    return call(
        exchanged_grad_kernel,
        [jax.ShapeDtypeStruct((features, hidden), jnp.bfloat16)],
        [rows, *rights],
        2 * blocks * chunks * slots * features * hidden,
        in_specs=[pl.BlockSpec((blocks, chunks, slots, tile), lambda i: (0, 0, 0, i))]
        + [pl.BlockSpec(a.shape, lambda i: (0, 0)) for a in rights],
        out_specs=[pl.BlockSpec((tile, hidden), lambda i: (i, 0))],
        grid=(features // tile,),
    )[0]


def add_kernel(into_ref, more_ref, out_ref):
    out_ref[...] = (
        into_ref[...].astype(jnp.float32) + more_ref[...].astype(jnp.float32)
    ).astype(jnp.bfloat16)


def add_half(into, more, which):
    half, features = more.shape
    place = pl.BlockSpec((half, features), lambda i: (which, 0))
    return call(
        add_kernel,
        [jax.ShapeDtypeStruct(into.shape, into.dtype)],
        [into, more],
        more.size,
        in_specs=[place, pl.BlockSpec((half, features), lambda i: (0, 0))],
        out_specs=[place],
        grid=(1,),
        input_output_aliases={0: 0},
    )[0]


def sum_kernel(one_ref, two_ref, three_ref, out_ref):
    out_ref[...] = (
        one_ref[...].astype(jnp.float32)
        + two_ref[...].astype(jnp.float32)
        + three_ref[...].astype(jnp.float32)
    ).astype(jnp.bfloat16)


def sum_three(one, two, three):
    return call(
        sum_kernel, [jax.ShapeDtypeStruct(one.shape, one.dtype)], [one, two, three], 2 * one.size
    )[0]


def forward_out_kernel(cap_rows, arrival_ref, gate_ref, route_ref, returned_ref, out_ref):
    total = None
    for k, t in enumerate(forward_targets(route_ref[...], cap_rows)):
        part = gate_ref[:, k : k + 1] * matmul(
            hits_of(t, returned_ref.shape[0]), returned_ref[...], ((1,), (0,))
        )
        total = part if total is None else total + part
    out_ref[...] = (arrival_ref[...].astype(jnp.float32) + total).astype(jnp.bfloat16)


def backward_out_kernel(
    cap_rows, saved_ref, gain_ref, cot_ref, route_ref, slot_ref, returned_ref, out_ref
):
    pick = sum(
        hits_of(t, returned_ref.shape[0]).astype(jnp.float32)
        for t in backward_targets(route_ref[...], slot_ref[...], cap_rows)
    ).astype(jnp.bfloat16)
    scaled = gain_ref[...] * matmul(pick, returned_ref[...], ((1,), (0,)))
    plain = saved_ref[...].astype(jnp.float32)
    recip = rms_scale(plain)
    cubed = recip * recip * recip
    out_ref[...] = (
        cot_ref[...].astype(jnp.float32)
        + recip * scaled
        - plain * cubed * jnp.mean(scaled * plain, axis=-1, keepdims=True)
    ).astype(jnp.bfloat16)


def body(
    fwd_handoff,
    saved_input,
    grad_handoff,
    gain,
    route_fwd,
    gate_fwd,
    route_bwd,
    slot_bwd,
    gate_bwd,
    w_in,
    w_out,
    saved_pre,
):
    groups = lax.axis_size("expert") // EXPERTS
    tok_rows, features = fwd_handoff.shape[1:]
    choices = route_fwd.shape[2]
    cap_rows = tok_rows * choices // EXPERTS
    all_rows = EXPERTS * cap_rows
    half = all_rows // 2
    mine = jnp.asarray(lax.axis_index("expert") % groups, jnp.int32).reshape(1)
    w_in_local = w_in[0]
    w_out_local = w_out[0]
    pre_blocks = saved_pre[0].reshape(EXPERTS, groups, cap_rows, -1)
    rows_shape = [jax.ShapeDtypeStruct((all_rows, features), jnp.bfloat16)]
    token_shape = [jax.ShapeDtypeStruct((tok_rows, features), jnp.bfloat16)]
    pick_flops = 2 * tok_rows * all_rows * features

    def send(values):
        return exchange(values.reshape(EXPERTS, -1, features), groups).reshape(-1, features)

    cotangent = shifted(grad_handoff, "section", -1)
    arrival = shifted(after(fwd_handoff, cotangent), "section", 1)[0]
    cotangent = cotangent[0]

    tagged = call(
        tagged_kernel,
        [jax.ShapeDtypeStruct((tok_rows, features + 128), jnp.bfloat16)],
        [saved_input[0], gain, route_bwd[0], slot_bwd[0]],
        0,
    )[0]
    tagged_left, tagged_right = turned(tagged, groups, 1), turned(tagged, groups, -1)
    tagged_left_top, tagged_right_bottom = cut_halves(tagged_left, tagged_right)
    tagged_top = turned(tagged_left_top, groups, 1)
    tagged_bottom = turned(tagged_right_bottom, groups, -1)

    grad_rows = call(
        functools.partial(pick_grad_kernel, cap_rows),
        rows_shape,
        [after(cotangent, tagged), gate_bwd[0], route_bwd[0], slot_bwd[0]],
        2 * pick_flops,
    )[0]
    rows_fwd = call(
        functools.partial(pick_forward_kernel, cap_rows),
        rows_shape,
        [after(arrival, tagged_top, tagged_bottom), gain, route_fwd[0]],
        pick_flops,
    )[0]

    grads = send(grad_rows)
    grads_left, grads_right = turned(grads, groups, 1), turned(grads, groups, -1)
    sent_fwd = send(after(rows_fwd, grads))
    whole, halves = (all_rows,), (half, half)
    hidden_0, pre_grad_0, back_0 = backward_chunks(
        mine, [grads], pre_blocks, w_in_local, w_out_local, [whole], (0,)
    )
    rows_bwd = call(
        functools.partial(picked_rows_kernel, choices),
        [jax.ShapeDtypeStruct((EXPERTS, groups, cap_rows, features), jnp.bfloat16)],
        [after(tagged, rows_fwd, *back_0), tagged_left, tagged_right, tagged_top, tagged_bottom],
        groups * pick_flops,
    )[0]
    grads_left_top, grads_right_bottom = cut_halves(after(grads_left, rows_bwd), grads_right)
    grads_top = turned(grads_left_top, groups, 1)
    grads_bottom = turned(grads_right_bottom, groups, -1)
    ready = after(sent_fwd, grads_left, grads_right)
    left, right = turned(ready, groups, 1), turned(ready, groups, -1)
    sent_rows = send(after(rows_bwd, sent_fwd, grads_left_top, grads_right_bottom))

    hidden_1, pre_grad_1, back_1 = backward_chunks(
        mine,
        [after(grads_left, sent_fwd), grads_right],
        pre_blocks,
        w_in_local,
        w_out_local,
        [whole] * 2,
        (groups - 1, 1),
    )
    hidden_2, pre_grad_2, back_2 = backward_chunks(
        mine,
        [after(grads_top, *back_1), grads_bottom],
        pre_blocks,
        w_in_local,
        w_out_local,
        [halves],
        (2,),
        split=True,
    )
    back_top = turned(back_2[0], groups, 1)
    back_bottom = turned(back_2[1], groups, -1)

    left_top, right_bottom = cut_halves(left, right)
    opposite_top = turned(left_top, groups, 1)
    opposite_bottom = turned(right_bottom, groups, -1)
    grad_w_out = weight_grad(
        [*hidden_0, *hidden_1, *hidden_2],
        [after(grads, left_top, right_bottom), grads_left, grads_right, grads_top, grads_bottom],
        256,
    )
    fwd_0 = forward_chunks([after(sent_fwd, left_top, right_bottom)], w_in_local, w_out_local, [whole])

    arrived = (grad_w_out, *fwd_0, opposite_top, opposite_bottom)
    back_to_left = add_half(back_1[1], after(back_top, *arrived), 0)
    back_to_right = add_half(back_1[0], after(back_bottom, *arrived), 1)
    back_left = turned(back_to_left, groups, 1)
    back_right = turned(back_to_right, groups, -1)
    fwd_1 = forward_chunks(
        [after(left, back_to_left, back_to_right), right], w_in_local, w_out_local, [whole] * 2
    )
    fwd_2 = forward_chunks(
        [after(opposite_top, *fwd_1), opposite_bottom], w_in_local, w_out_local, [halves], split=True
    )
    fwd_top = turned(fwd_2[0], groups, 1)
    fwd_bottom = turned(fwd_2[1], groups, -1)

    back_sum = sum_three(after(back_0[0], *fwd_2), back_left, back_right)
    fwd_to_left = add_half(fwd_1[1], fwd_top, 0)
    fwd_to_right = add_half(fwd_1[0], fwd_bottom, 1)
    return_bwd = send(after(back_sum, sent_rows, fwd_to_left, fwd_to_right))
    grad_w_in = exchanged_grad(
        sent_rows.reshape(rows_bwd.shape), [*pre_grad_0, *pre_grad_1, *pre_grad_2], 256
    )

    fwd_left = turned(fwd_to_left, groups, 1)
    fwd_right = turned(fwd_to_right, groups, -1)
    fwd_sum = sum_three(fwd_0[0], after(fwd_left, grad_w_in), fwd_right)
    return_fwd = send(after(fwd_sum, return_bwd))

    section_out = call(
        functools.partial(forward_out_kernel, cap_rows),
        token_shape,
        [arrival, gate_fwd[0], route_fwd[0], return_fwd],
        2 * pick_flops,
    )[0]
    input_grad = call(
        functools.partial(backward_out_kernel, cap_rows),
        token_shape,
        [saved_input[0], gain, cotangent, route_bwd[0], slot_bwd[0], return_bwd],
        pick_flops,
    )[0]
    return (section_out[None], input_grad[None], grad_w_in[None], grad_w_out[None])


def solution(mesh):
    placed = (
        P("section", "expert", None),
        P("section", "expert", None),
        P("section", "expert", None),
        P("section", None),
        P("section", "expert", None),
        P("section", "expert", None),
        P("section", "expert", None),
        P("section", "expert", None),
        P("section", "expert", None),
        P("section", None, "expert"),
        P("section", "expert", None),
        P("section", "expert", None),
    )
    return jax.shard_map(
        body,
        mesh=mesh,
        in_specs=placed,
        out_specs=(
            P("section", "expert", None),
            P("section", "expert", None),
            P("section", None, "expert"),
            P("section", "expert", None),
        ),
        check_vma=False,
    )
```

```python
import functools

import jax
import jax.numpy as jnp
from jax import lax
from jax.experimental import pallas as pl
from jax.experimental.pallas import tpu as pltpu
from jax.sharding import PartitionSpec as P

EXPERTS = 8


EPSILON = 1e-06
TANH_SCALE = 0.7978845608028654
CUBIC_COEF = 0.044715


def shifted(block, axis, distance):
    devices = range(lax.axis_size(axis))
    route = [((i - distance) % len(devices), i) for i in devices]
    return lax.ppermute(block, axis, route)


def turned(block, groups, distance):
    route = [
        (e * groups + g, e * groups + (g + distance) % groups)
        for e in range(EXPERTS)
        for g in range(groups)
    ]
    return lax.ppermute(block, "expert", route)


def exchange(block, groups):
    index_groups = [[e * groups + g for e in range(EXPERTS)] for g in range(groups)]
    return lax.all_to_all(
        block, "expert", split_axis=0, concat_axis=0, tiled=True, axis_index_groups=index_groups
    )


def after(value, *earlier):
    return lax.optimization_barrier((value, *earlier))[0]


def after(value, *earlier):
    return lax.optimization_barrier((value, *earlier))[0]


VMEM_BYTES = 30 * 1024 * 1024


def matmul(left, right, dims):
    return lax.dot_general(left, right, (dims, ((), ())), preferred_element_type=jnp.float32)


def call(kernel, out_shapes, operands, flops, in_specs=None, out_specs=None, **more):
    moved = sum(a.size * a.dtype.itemsize for a in operands)
    moved += sum(o.size * o.dtype.itemsize for o in out_shapes)
    if in_specs is None and "grid_spec" not in more:

        def whole(array):
            return pl.BlockSpec(array.shape, lambda i: (0,) * len(array.shape))

        more["grid"] = (1,)
        more["in_specs"] = [whole(a) for a in operands]
        more["out_specs"] = [whole(o) for o in out_shapes]
    elif in_specs is not None:
        more["in_specs"] = in_specs
        more["out_specs"] = out_specs
    return pl.pallas_call(
        kernel,
        out_shape=out_shapes,
        cost_estimate=pl.CostEstimate(flops=flops, bytes_accessed=moved, transcendentals=0),
        compiler_params=pltpu.CompilerParams(vmem_limit_bytes=VMEM_BYTES),
        **more,
    )(*operands)


def rms_scale(widened):
    return lax.rsqrt(jnp.mean(widened * widened, axis=-1, keepdims=True) + EPSILON)


def normed_of(tokens_ref, gain_ref):
    widened = tokens_ref[...].astype(jnp.float32)
    return (widened * rms_scale(widened) * gain_ref[...]).astype(jnp.bfloat16)


def hits_of(target, rows):
    ids = lax.broadcasted_iota(jnp.int32, (target.shape[0], rows), 1)
    return (target == ids).astype(jnp.float32).astype(jnp.bfloat16)


def forward_targets(route, cap_rows):
    tokens, choices = route.shape
    lanes = lax.broadcasted_iota(jnp.int32, (tokens, 128), 1)
    below = (
        lax.broadcasted_iota(jnp.int32, (tokens, tokens), 0)
        > lax.broadcasted_iota(jnp.int32, (tokens, tokens), 1)
    ).astype(jnp.float32)
    below = below.astype(jnp.bfloat16)
    ahead = jnp.zeros((1, 128), jnp.float32)
    targets = []
    for k in range(choices):
        expert = route[:, k : k + 1]
        named = (expert == lanes).astype(jnp.float32)
        count = matmul(below, named.astype(jnp.bfloat16), ((1,), (0,))) + ahead
        rank = jnp.sum(named * count, axis=1, keepdims=True).astype(jnp.int32)
        targets.append(expert * cap_rows + rank)
        ahead = ahead + jnp.sum(named, axis=0, keepdims=True)
    return targets


def backward_targets(route, slot, cap_rows):
    target = route * cap_rows + slot
    return [target[:, k : k + 1] for k in range(target.shape[1])]


def pick_forward_kernel(cap_rows, tokens_ref, gain_ref, route_ref, out_ref):
    normed = normed_of(tokens_ref, gain_ref)
    pick = sum(
        hits_of(t, out_ref.shape[0]).astype(jnp.float32)
        for t in forward_targets(route_ref[...], cap_rows)
    ).astype(jnp.bfloat16)
    out_ref[...] = matmul(pick, normed, ((0,), (0,))).astype(jnp.bfloat16)


def tagged_kernel(tokens_ref, gain_ref, route_ref, slot_ref, out_ref):
    tokens, features = tokens_ref.shape
    choices = route_ref.shape[1]
    out_ref[:, :features] = normed_of(tokens_ref, gain_ref)
    lanes = lax.broadcasted_iota(jnp.int32, (tokens, out_ref.shape[1] - features), 1)
    tags = jnp.zeros(lanes.shape, jnp.int32)
    for k in range(choices):
        tags = jnp.where(lanes == k, route_ref[:, k : k + 1], tags)
        tags = jnp.where(lanes == choices + k, slot_ref[:, k : k + 1], tags)
    out_ref[:, features:] = tags.astype(jnp.float32).astype(jnp.bfloat16)


def picked_rows_kernel(choices, own_ref, left_ref, right_ref, top_ref, bottom_ref, out_ref):
    experts, _, cap_rows, features = out_ref.shape
    for c, pieces in enumerate(((own_ref,), (left_ref,), (right_ref,), (top_ref, bottom_ref))):
        rows = None
        for ref in pieces:
            tags = ref[:, features:].astype(jnp.float32).astype(jnp.int32)
            pick = None
            for k in range(choices):
                target = tags[:, k : k + 1] * cap_rows + tags[:, choices + k : choices + k + 1]
                hit = hits_of(target, experts * cap_rows).astype(jnp.float32)
                pick = hit if pick is None else pick + hit
            part = matmul(pick.astype(jnp.bfloat16), ref[:, :features], ((0,), (0,)))
            rows = part if rows is None else rows + part
        out_ref[:, c] = rows.astype(jnp.bfloat16).reshape(experts, cap_rows, features)


def cut_kernel(left_ref, right_ref, top_ref, bottom_ref, sems):
    half = top_ref.shape[0]
    copies = [
        pltpu.make_async_copy(left_ref.at[:half], top_ref, sems.at[0]),
        pltpu.make_async_copy(right_ref.at[half:], bottom_ref, sems.at[1]),
    ]
    for copy in copies:
        copy.start()
    for copy in copies:
        copy.wait()


def cut_halves(left, right):
    anywhere = pl.BlockSpec(memory_space=pl.ANY)
    return call(
        cut_kernel,
        [jax.ShapeDtypeStruct((left.shape[0] // 2, left.shape[1]), left.dtype)] * 2,
        [left, right],
        0,
        in_specs=[anywhere] * 2,
        out_specs=[pl.BlockSpec(memory_space=pltpu.VMEM)] * 2,
        scratch_shapes=[pltpu.SemaphoreType.DMA((2,))],
    )


def pick_grad_kernel(cap_rows, cot_ref, gate_ref, route_ref, slot_ref, out_ref):
    cot = cot_ref[...].astype(jnp.float32)
    total = None
    for k, t in enumerate(backward_targets(route_ref[...], slot_ref[...], cap_rows)):
        gated = (gate_ref[:, k : k + 1] * cot).astype(jnp.bfloat16)
        part = matmul(hits_of(t, out_ref.shape[0]), gated, ((0,), (0,)))
        total = part if total is None else total + part
    out_ref[...] = total.astype(jnp.bfloat16)


def backward_kernel(sizes, split, place_ref, w_in_ref, w_out_ref, *refs):
    chunks = len(sizes)
    pieces = sum(len(s) for s in sizes)
    grads = list(refs[:pieces])
    pres = refs[pieces : pieces + chunks]
    outs = refs[pieces + chunks :]
    hidden_refs = outs[:chunks]
    pre_grad_refs = outs[chunks : 2 * chunks]
    back_refs = outs[2 * chunks : -1]
    wide = outs[-1]
    for c in range(chunks):
        row = 0
        for size in sizes[c]:
            wide[row : row + size, :] = matmul(grads.pop(0)[...], w_out_ref[...], ((1,), (1,)))
            row += size
        blocks, _, slots, _ = pres[c].shape
        for b in range(blocks):
            span = slice(b * slots, (b + 1) * slots)
            pre = pres[c][b, 0].astype(jnp.float32)
            square = pre * pre
            inner = TANH_SCALE * (pre + CUBIC_COEF * square * pre)
            tangent = jnp.tanh(inner)
            half = 0.5 * (1.0 + tangent)
            derivative = half + 0.5 * pre * (1.0 - tangent * tangent) * TANH_SCALE * (
                1.0 + 3.0 * CUBIC_COEF * square
            )
            hidden_refs[c][span, :] = (pre * half).astype(jnp.bfloat16)
            pre_grad_refs[c][span, :] = (wide[span, :] * derivative).astype(jnp.bfloat16)
        parts = 2 if split else 1
        for h in range(parts):
            span = slice(h * row // parts, (h + 1) * row // parts)
            back_refs[parts * c + h][...] = matmul(
                pre_grad_refs[c][span, :], w_in_ref[...], ((1,), (1,))
            ).astype(jnp.bfloat16)


def forward_kernel(sizes, split, w_in_ref, w_out_ref, *refs):
    chunks = len(sizes)
    pieces = sum(len(s) for s in sizes)
    rows = list(refs[:pieces])
    outs = refs[pieces:-2]
    wide, hidden = refs[-2:]
    for c in range(chunks):
        row = 0
        for size in sizes[c]:
            wide[row : row + size, :] = matmul(rows.pop(0)[...], w_in_ref[...], ((1,), (0,)))
            row += size
        for b in range(row // 32):
            span = slice(b * 32, (b + 1) * 32)
            pre = wide[span, :]
            tangent = jnp.tanh(TANH_SCALE * (pre + CUBIC_COEF * pre * pre * pre))
            hidden[span, :] = (0.5 * pre * (1.0 + tangent)).astype(jnp.bfloat16)
        parts = 2 if split else 1
        for h in range(parts):
            span = slice(h * row // parts, (h + 1) * row // parts)
            outs[parts * c + h][...] = matmul(
                hidden[span, :], w_out_ref[...], ((1,), (0,))
            ).astype(jnp.bfloat16)


def backward_chunks(place, grads, pre_blocks, w_in, w_out, sizes, shifts, split=False):
    experts, groups, cap_rows, hidden = pre_blocks.shape
    features = w_in.shape[0]
    rows = experts * cap_rows
    chunks = len(shifts)
    parts = 2 if split else 1

    def whole(shape):
        return pl.BlockSpec(shape, lambda i, p: (0,) * len(shape))

    def shared(shift):
        return pl.BlockSpec(
            (experts, 1, cap_rows, hidden),
            lambda i, p: (0, lax.rem(p[0] + shift, groups), 0, 0),
        )

    out_shapes = [jax.ShapeDtypeStruct((rows, hidden), jnp.bfloat16)] * (2 * chunks) + [
        jax.ShapeDtypeStruct((rows // parts, features), jnp.bfloat16)
    ] * (parts * chunks)
    outs = call(
        functools.partial(backward_kernel, sizes, split),
        out_shapes,
        [place, w_in, w_out, *grads] + [pre_blocks] * chunks,
        4 * chunks * rows * hidden * features,
        grid_spec=pltpu.PrefetchScalarGridSpec(
            num_scalar_prefetch=1,
            grid=(1,),
            in_specs=[whole(w_in.shape), whole(w_out.shape)]
            + [whole(g.shape) for g in grads]
            + [shared(s) for s in shifts],
            out_specs=[whole(o.shape) for o in out_shapes],
            scratch_shapes=[pltpu.VMEM((rows, hidden), jnp.float32)],
        ),
    )
    return outs[:chunks], outs[chunks : 2 * chunks], outs[2 * chunks :]


def forward_chunks(rows_list, w_in, w_out, sizes, split=False):
    features, hidden = w_in.shape
    rows = sum(sizes[0])
    parts = 2 if split else 1
    return call(
        functools.partial(forward_kernel, sizes, split),
        [jax.ShapeDtypeStruct((rows // parts, features), jnp.bfloat16)] * (parts * len(sizes)),
        [w_in, w_out, *rows_list],
        4 * len(sizes) * rows * hidden * features,
        scratch_shapes=[
            pltpu.VMEM((rows, hidden), jnp.float32),
            pltpu.VMEM((rows, hidden), jnp.bfloat16),
        ],
    )


def weight_grad_kernel(lefts, rights, *refs):
    out_ref = refs[-1]

    def cut(pieces, sizes):
        spans, at = [], 0
        for ref, size in zip(pieces, sizes):
            spans.append((at, at + size, ref))
            at += size
        return spans

    left_spans = cut(refs[: len(lefts)], lefts)
    right_spans = cut(refs[len(lefts) : -1], rights)
    total = None
    for start, end, left in left_spans:
        for first, last, right in right_spans:
            low, high = max(start, first), min(end, last)
            if low >= high:
                continue
            part = matmul(
                left[low - start : high - start, :],
                right[low - first : high - first, :],
                ((0,), (0,)),
            )
            total = part if total is None else total + part
    out_ref[...] = total.astype(jnp.bfloat16)


def weight_grad(lefts, rights, tile):
    left_cols, right_cols = lefts[0].shape[1], rights[0].shape[1]
    rows = sum(a.shape[0] for a in lefts)
    return call(
        functools.partial(
            weight_grad_kernel, [a.shape[0] for a in lefts], [a.shape[0] for a in rights]
        ),
        [jax.ShapeDtypeStruct((left_cols, right_cols), jnp.bfloat16)],
        [*lefts, *rights],
        2 * rows * left_cols * right_cols,
        in_specs=[pl.BlockSpec((a.shape[0], tile), lambda i: (0, i)) for a in lefts]
        + [pl.BlockSpec(a.shape, lambda i: (0, 0)) for a in rights],
        out_specs=[pl.BlockSpec((tile, right_cols), lambda i: (i, 0))],
        grid=(left_cols // tile,),
    )[0]


def exchanged_grad_kernel(rows_ref, *refs):
    out_ref = refs[-1]
    blocks, chunks, slots, tile = rows_ref.shape
    total = None
    for c in range(chunks):
        rows = rows_ref[:, c].reshape(blocks * slots, tile)
        part = matmul(rows, refs[c][...], ((0,), (0,)))
        total = part if total is None else total + part
    out_ref[...] = total.astype(jnp.bfloat16)


def exchanged_grad(rows, rights, tile):
    blocks, chunks, slots, features = rows.shape
    hidden = rights[0].shape[1]
    return call(
        exchanged_grad_kernel,
        [jax.ShapeDtypeStruct((features, hidden), jnp.bfloat16)],
        [rows, *rights],
        2 * blocks * chunks * slots * features * hidden,
        in_specs=[pl.BlockSpec((blocks, chunks, slots, tile), lambda i: (0, 0, 0, i))]
        + [pl.BlockSpec(a.shape, lambda i: (0, 0)) for a in rights],
        out_specs=[pl.BlockSpec((tile, hidden), lambda i: (i, 0))],
        grid=(features // tile,),
    )[0]


def add_kernel(into_ref, more_ref, out_ref):
    out_ref[...] = (
        into_ref[...].astype(jnp.float32) + more_ref[...].astype(jnp.float32)
    ).astype(jnp.bfloat16)


def add_half(into, more, which):
    half, features = more.shape
    place = pl.BlockSpec((half, features), lambda i: (which, 0))
    return call(
        add_kernel,
        [jax.ShapeDtypeStruct(into.shape, into.dtype)],
        [into, more],
        more.size,
        in_specs=[place, pl.BlockSpec((half, features), lambda i: (0, 0))],
        out_specs=[place],
        grid=(1,),
        input_output_aliases={0: 0},
    )[0]


def sum_kernel(one_ref, two_ref, three_ref, out_ref):
    out_ref[...] = (
        one_ref[...].astype(jnp.float32)
        + two_ref[...].astype(jnp.float32)
        + three_ref[...].astype(jnp.float32)
    ).astype(jnp.bfloat16)


def sum_three(one, two, three):
    return call(
        sum_kernel, [jax.ShapeDtypeStruct(one.shape, one.dtype)], [one, two, three], 2 * one.size
    )[0]


def forward_out_kernel(cap_rows, arrival_ref, gate_ref, route_ref, returned_ref, out_ref):
    total = None
    for k, t in enumerate(forward_targets(route_ref[...], cap_rows)):
        part = gate_ref[:, k : k + 1] * matmul(
            hits_of(t, returned_ref.shape[0]), returned_ref[...], ((1,), (0,))
        )
        total = part if total is None else total + part
    out_ref[...] = (arrival_ref[...].astype(jnp.float32) + total).astype(jnp.bfloat16)


def backward_out_kernel(
    cap_rows, saved_ref, gain_ref, cot_ref, route_ref, slot_ref, returned_ref, out_ref
):
    pick = sum(
        hits_of(t, returned_ref.shape[0]).astype(jnp.float32)
        for t in backward_targets(route_ref[...], slot_ref[...], cap_rows)
    ).astype(jnp.bfloat16)
    scaled = gain_ref[...] * matmul(pick, returned_ref[...], ((1,), (0,)))
    plain = saved_ref[...].astype(jnp.float32)
    recip = rms_scale(plain)
    cubed = recip * recip * recip
    out_ref[...] = (
        cot_ref[...].astype(jnp.float32)
        + recip * scaled
        - plain * cubed * jnp.mean(scaled * plain, axis=-1, keepdims=True)
    ).astype(jnp.bfloat16)


def body(
    fwd_handoff,
    saved_input,
    grad_handoff,
    gain,
    route_fwd,
    gate_fwd,
    route_bwd,
    slot_bwd,
    gate_bwd,
    w_in,
    w_out,
    saved_pre,
):
    groups = lax.axis_size("expert") // EXPERTS
    tok_rows, features = fwd_handoff.shape[1:]
    choices = route_fwd.shape[2]
    cap_rows = tok_rows * choices // EXPERTS
    all_rows = EXPERTS * cap_rows
    half = all_rows // 2
    mine = jnp.asarray(lax.axis_index("expert") % groups, jnp.int32).reshape(1)
    w_in_local = w_in[0]
    w_out_local = w_out[0]
    pre_blocks = saved_pre[0].reshape(EXPERTS, groups, cap_rows, -1)
    rows_shape = [jax.ShapeDtypeStruct((all_rows, features), jnp.bfloat16)]
    token_shape = [jax.ShapeDtypeStruct((tok_rows, features), jnp.bfloat16)]
    pick_flops = 2 * tok_rows * all_rows * features

    def send(values):
        return exchange(values.reshape(EXPERTS, -1, features), groups).reshape(-1, features)

    cotangent = shifted(grad_handoff, "section", -1)
    arrival = shifted(after(fwd_handoff, cotangent), "section", 1)[0]
    cotangent = cotangent[0]

    tagged = call(
        tagged_kernel,
        [jax.ShapeDtypeStruct((tok_rows, features + 128), jnp.bfloat16)],
        [saved_input[0], gain, route_bwd[0], slot_bwd[0]],
        0,
    )[0]
    tagged_left, tagged_right = turned(tagged, groups, 1), turned(tagged, groups, -1)
    tagged_left_top, tagged_right_bottom = cut_halves(tagged_left, tagged_right)
    tagged_top = turned(tagged_left_top, groups, 1)
    tagged_bottom = turned(tagged_right_bottom, groups, -1)

    grad_rows = call(
        functools.partial(pick_grad_kernel, cap_rows),
        rows_shape,
        [after(cotangent, tagged), gate_bwd[0], route_bwd[0], slot_bwd[0]],
        2 * pick_flops,
    )[0]
    rows_fwd = call(
        functools.partial(pick_forward_kernel, cap_rows),
        rows_shape,
        [after(arrival, tagged_top, tagged_bottom), gain, route_fwd[0]],
        pick_flops,
    )[0]

    grads = send(grad_rows)
    grads_left, grads_right = turned(grads, groups, 1), turned(grads, groups, -1)
    sent_fwd = send(after(rows_fwd, grads))
    whole, halves = (all_rows,), (half, half)
    hidden_0, pre_grad_0, back_0 = backward_chunks(
        mine, [grads], pre_blocks, w_in_local, w_out_local, [whole], (0,)
    )
    rows_bwd = call(
        functools.partial(picked_rows_kernel, choices),
        [jax.ShapeDtypeStruct((EXPERTS, groups, cap_rows, features), jnp.bfloat16)],
        [after(tagged, rows_fwd, *back_0), tagged_left, tagged_right, tagged_top, tagged_bottom],
        groups * pick_flops,
    )[0]
    grads_left_top, grads_right_bottom = cut_halves(after(grads_left, rows_bwd), grads_right)
    grads_top = turned(grads_left_top, groups, 1)
    grads_bottom = turned(grads_right_bottom, groups, -1)
    ready = after(sent_fwd, grads_left, grads_right)
    left, right = turned(ready, groups, 1), turned(ready, groups, -1)
    sent_rows = send(after(rows_bwd, sent_fwd, grads_left_top, grads_right_bottom))

    hidden_1, pre_grad_1, back_1 = backward_chunks(
        mine,
        [after(grads_left, sent_fwd), grads_right],
        pre_blocks,
        w_in_local,
        w_out_local,
        [whole] * 2,
        (groups - 1, 1),
    )
    hidden_2, pre_grad_2, back_2 = backward_chunks(
        mine,
        [after(grads_top, *back_1), grads_bottom],
        pre_blocks,
        w_in_local,
        w_out_local,
        [halves],
        (2,),
        split=True,
    )
    back_top = turned(back_2[0], groups, 1)
    back_bottom = turned(back_2[1], groups, -1)

    left_top, right_bottom = cut_halves(left, right)
    opposite_top = turned(left_top, groups, 1)
    opposite_bottom = turned(right_bottom, groups, -1)
    grad_w_out = weight_grad(
        [*hidden_0, *hidden_1, *hidden_2],
        [after(grads, left_top, right_bottom), grads_left, grads_right, grads_top, grads_bottom],
        256,
    )
    fwd_0 = forward_chunks([after(sent_fwd, left_top, right_bottom)], w_in_local, w_out_local, [whole])

    arrived = (grad_w_out, *fwd_0, opposite_top, opposite_bottom)
    back_to_left = add_half(back_1[1], after(back_top, *arrived), 0)
    back_to_right = add_half(back_1[0], after(back_bottom, *arrived), 1)
    back_left = turned(back_to_left, groups, 1)
    back_right = turned(back_to_right, groups, -1)
    fwd_1 = forward_chunks(
        [after(left, back_to_left, back_to_right), right], w_in_local, w_out_local, [whole] * 2
    )
    fwd_2 = forward_chunks(
        [after(opposite_top, *fwd_1), opposite_bottom], w_in_local, w_out_local, [halves], split=True
    )
    fwd_top = turned(fwd_2[0], groups, 1)
    fwd_bottom = turned(fwd_2[1], groups, -1)

    back_sum = sum_three(after(back_0[0], *fwd_2), back_left, back_right)
    fwd_to_left = add_half(fwd_1[1], fwd_top, 0)
    fwd_to_right = add_half(fwd_1[0], fwd_bottom, 1)
    return_bwd = send(after(back_sum, sent_rows, fwd_to_left, fwd_to_right))
    grad_w_in = exchanged_grad(
        sent_rows.reshape(rows_bwd.shape), [*pre_grad_0, *pre_grad_1, *pre_grad_2], 256
    )

    fwd_left = turned(fwd_to_left, groups, 1)
    fwd_right = turned(fwd_to_right, groups, -1)
    fwd_sum = sum_three(fwd_0[0], after(fwd_left, grad_w_in), fwd_right)
    return_fwd = send(after(fwd_sum, return_bwd))

    section_out = call(
        functools.partial(forward_out_kernel, cap_rows),
        token_shape,
        [arrival, gate_fwd[0], route_fwd[0], return_fwd],
        2 * pick_flops,
    )[0]
    input_grad = call(
        functools.partial(backward_out_kernel, cap_rows),
        token_shape,
        [saved_input[0], gain, cotangent, route_bwd[0], slot_bwd[0], return_bwd],
        pick_flops,
    )[0]
    return (section_out[None], input_grad[None], grad_w_in[None], grad_w_out[None])


def solution(mesh):
    placed = (
        P("section", "expert", None),
        P("section", "expert", None),
        P("section", "expert", None),
        P("section", None),
        P("section", "expert", None),
        P("section", "expert", None),
        P("section", "expert", None),
        P("section", "expert", None),
        P("section", "expert", None),
        P("section", None, "expert"),
        P("section", "expert", None),
        P("section", "expert", None),
    )
    return jax.shard_map(
        body,
        mesh=mesh,
        in_specs=placed,
        out_specs=(
            P("section", "expert", None),
            P("section", "expert", None),
            P("section", None, "expert"),
            P("section", "expert", None),
        ),
        check_vma=False,
    )
```

```python
import functools

import jax
import jax.numpy as jnp
from jax import lax
from jax.experimental import pallas as pl
from jax.experimental.pallas import tpu as pltpu
from jax.sharding import PartitionSpec as P

EXPERTS = 8


EPSILON = 1e-06
TANH_SCALE = 0.7978845608028654
CUBIC_COEF = 0.044715


def shifted(block, axis, distance):
    devices = range(lax.axis_size(axis))
    route = [((i - distance) % len(devices), i) for i in devices]
    return lax.ppermute(block, axis, route)


def turned(block, groups, distance):
    route = [
        (e * groups + g, e * groups + (g + distance) % groups)
        for e in range(EXPERTS)
        for g in range(groups)
    ]
    return lax.ppermute(block, "expert", route)


def exchange(block, groups):
    index_groups = [[e * groups + g for e in range(EXPERTS)] for g in range(groups)]
    return lax.all_to_all(
        block, "expert", split_axis=0, concat_axis=0, tiled=True, axis_index_groups=index_groups
    )


def after(value, *earlier):
    return lax.optimization_barrier((value, *earlier))[0]


def after(value, *earlier):
    return lax.optimization_barrier((value, *earlier))[0]


VMEM_BYTES = 30 * 1024 * 1024


def matmul(left, right, dims):
    return lax.dot_general(left, right, (dims, ((), ())), preferred_element_type=jnp.float32)


ANYWHERE = pl.BlockSpec(memory_space=pl.ANY)
IN_VMEM = pl.BlockSpec(memory_space=pltpu.VMEM)
TOKEN = jax.ShapeDtypeStruct((8, 128), jnp.float32)


def call(kernel, out_shapes, operands, flops, in_specs=None, out_specs=None, waits=(), **more):
    moved = sum(a.size * a.dtype.itemsize for a in operands)
    moved += sum(o.size * o.dtype.itemsize for o in out_shapes)
    taken, extra, given = len(operands), len(waits), len(out_shapes)

    def run(*refs):
        rest = refs[taken + extra :]
        kernel(*refs[:taken], *rest[:given], *rest[given + 1 :])
        rest[given][...] = jnp.zeros(TOKEN.shape, TOKEN.dtype)

    if in_specs is None and "grid_spec" not in more:

        def whole(array):
            return pl.BlockSpec(array.shape, lambda i: (0,) * len(array.shape))

        more["grid"] = (1,)
        in_specs = [whole(a) for a in operands]
        out_specs = [whole(o) for o in out_shapes]
    if in_specs is not None:
        more["in_specs"] = [*in_specs, *[ANYWHERE] * extra]
        more["out_specs"] = [*out_specs, IN_VMEM]
    *outs, token = pl.pallas_call(
        run,
        out_shape=[*out_shapes, TOKEN],
        cost_estimate=pl.CostEstimate(flops=flops, bytes_accessed=moved, transcendentals=0),
        compiler_params=pltpu.CompilerParams(vmem_limit_bytes=VMEM_BYTES),
        **more,
    )(*operands, *waits)
    return outs, token


def rms_scale(widened):
    return lax.rsqrt(jnp.mean(widened * widened, axis=-1, keepdims=True) + EPSILON)


def normed_of(tokens_ref, gain_ref):
    widened = tokens_ref[...].astype(jnp.float32)
    return (widened * rms_scale(widened) * gain_ref[...]).astype(jnp.bfloat16)


def hits_of(target, rows):
    ids = lax.broadcasted_iota(jnp.int32, (target.shape[0], rows), 1)
    return (target == ids).astype(jnp.float32).astype(jnp.bfloat16)


def forward_targets(route, cap_rows):
    tokens, choices = route.shape
    lanes = lax.broadcasted_iota(jnp.int32, (tokens, 128), 1)
    below = (
        lax.broadcasted_iota(jnp.int32, (tokens, tokens), 0)
        > lax.broadcasted_iota(jnp.int32, (tokens, tokens), 1)
    ).astype(jnp.float32)
    below = below.astype(jnp.bfloat16)
    ahead = jnp.zeros((1, 128), jnp.float32)
    targets = []
    for k in range(choices):
        expert = route[:, k : k + 1]
        named = (expert == lanes).astype(jnp.float32)
        count = matmul(below, named.astype(jnp.bfloat16), ((1,), (0,))) + ahead
        rank = jnp.sum(named * count, axis=1, keepdims=True).astype(jnp.int32)
        targets.append(expert * cap_rows + rank)
        ahead = ahead + jnp.sum(named, axis=0, keepdims=True)
    return targets


def backward_targets(route, slot, cap_rows):
    target = route * cap_rows + slot
    return [target[:, k : k + 1] for k in range(target.shape[1])]


def pick_forward_kernel(cap_rows, tokens_ref, gain_ref, route_ref, out_ref):
    normed = normed_of(tokens_ref, gain_ref)
    pick = sum(
        hits_of(t, out_ref.shape[0]).astype(jnp.float32)
        for t in forward_targets(route_ref[...], cap_rows)
    ).astype(jnp.bfloat16)
    out_ref[...] = matmul(pick, normed, ((0,), (0,))).astype(jnp.bfloat16)


def tagged_kernel(tokens_ref, gain_ref, route_ref, slot_ref, out_ref):
    tokens, features = tokens_ref.shape
    choices = route_ref.shape[1]
    out_ref[:, :features] = normed_of(tokens_ref, gain_ref)
    lanes = lax.broadcasted_iota(jnp.int32, (tokens, out_ref.shape[1] - features), 1)
    tags = jnp.zeros(lanes.shape, jnp.int32)
    for k in range(choices):
        tags = jnp.where(lanes == k, route_ref[:, k : k + 1], tags)
        tags = jnp.where(lanes == choices + k, slot_ref[:, k : k + 1], tags)
    out_ref[:, features:] = tags.astype(jnp.float32).astype(jnp.bfloat16)


def picked_rows_kernel(choices, own_ref, left_ref, out_ref):
    experts, _, cap_rows, features = out_ref.shape
    for c, ref in enumerate((own_ref, left_ref)):
        tags = ref[:, features:].astype(jnp.float32).astype(jnp.int32)
        pick = None
        for k in range(choices):
            target = tags[:, k : k + 1] * cap_rows + tags[:, choices + k : choices + k + 1]
            hit = hits_of(target, experts * cap_rows).astype(jnp.float32)
            pick = hit if pick is None else pick + hit
        rows = matmul(pick.astype(jnp.bfloat16), ref[:, :features], ((0,), (0,)))
        out_ref[:, c] = rows.astype(jnp.bfloat16).reshape(experts, cap_rows, features)


def cut_kernel(left_ref, right_ref, top_ref, bottom_ref, sems):
    half = top_ref.shape[0]
    copies = [
        pltpu.make_async_copy(left_ref.at[:half], top_ref, sems.at[0]),
        pltpu.make_async_copy(right_ref.at[half:], bottom_ref, sems.at[1]),
    ]
    for copy in copies:
        copy.start()
    for copy in copies:
        copy.wait()


def cut_halves(left, right, waits=()):
    outs, token = call(
        cut_kernel,
        [jax.ShapeDtypeStruct((left.shape[0] // 2, left.shape[1]), left.dtype)] * 2,
        [left, right],
        0,
        in_specs=[ANYWHERE] * 2,
        out_specs=[IN_VMEM] * 2,
        scratch_shapes=[pltpu.SemaphoreType.DMA((2,))],
        waits=waits,
    )
    return outs[0], outs[1], token


def pick_grad_kernel(cap_rows, cot_ref, gate_ref, route_ref, slot_ref, out_ref):
    cot = cot_ref[...].astype(jnp.float32)
    total = None
    for k, t in enumerate(backward_targets(route_ref[...], slot_ref[...], cap_rows)):
        gated = (gate_ref[:, k : k + 1] * cot).astype(jnp.bfloat16)
        part = matmul(hits_of(t, out_ref.shape[0]), gated, ((0,), (0,)))
        total = part if total is None else total + part
    out_ref[...] = total.astype(jnp.bfloat16)


def backward_kernel(sizes, split, place_ref, w_in_ref, w_out_ref, *refs):
    chunks = len(sizes)
    pieces = sum(len(s) for s in sizes)
    grads = list(refs[:pieces])
    pres = refs[pieces : pieces + chunks]
    outs = refs[pieces + chunks :]
    hidden_refs = outs[:chunks]
    pre_grad_refs = outs[chunks : 2 * chunks]
    back_refs = outs[2 * chunks : -1]
    wide = outs[-1]
    for c in range(chunks):
        row = 0
        for size in sizes[c]:
            wide[row : row + size, :] = matmul(grads.pop(0)[...], w_out_ref[...], ((1,), (1,)))
            row += size
        blocks, _, slots, _ = pres[c].shape
        for b in range(blocks):
            span = slice(b * slots, (b + 1) * slots)
            pre = pres[c][b, 0].astype(jnp.float32)
            square = pre * pre
            inner = TANH_SCALE * (pre + CUBIC_COEF * square * pre)
            tangent = jnp.tanh(inner)
            half = 0.5 * (1.0 + tangent)
            derivative = half + 0.5 * pre * (1.0 - tangent * tangent) * TANH_SCALE * (
                1.0 + 3.0 * CUBIC_COEF * square
            )
            hidden_refs[c][span, :] = (pre * half).astype(jnp.bfloat16)
            pre_grad_refs[c][span, :] = (wide[span, :] * derivative).astype(jnp.bfloat16)
        parts = 2 if split else 1
        for h in range(parts):
            span = slice(h * row // parts, (h + 1) * row // parts)
            back_refs[parts * c + h][...] = matmul(
                pre_grad_refs[c][span, :], w_in_ref[...], ((1,), (1,))
            ).astype(jnp.bfloat16)


def forward_kernel(sizes, split, w_in_ref, w_out_ref, *refs):
    chunks = len(sizes)
    pieces = sum(len(s) for s in sizes)
    rows = list(refs[:pieces])
    outs = refs[pieces:-2]
    wide, hidden = refs[-2:]
    for c in range(chunks):
        row = 0
        for size in sizes[c]:
            wide[row : row + size, :] = matmul(rows.pop(0)[...], w_in_ref[...], ((1,), (0,)))
            row += size
        for b in range(row // 32):
            span = slice(b * 32, (b + 1) * 32)
            pre = wide[span, :]
            tangent = jnp.tanh(TANH_SCALE * (pre + CUBIC_COEF * pre * pre * pre))
            hidden[span, :] = (0.5 * pre * (1.0 + tangent)).astype(jnp.bfloat16)
        parts = 2 if split else 1
        for h in range(parts):
            span = slice(h * row // parts, (h + 1) * row // parts)
            outs[parts * c + h][...] = matmul(
                hidden[span, :], w_out_ref[...], ((1,), (0,))
            ).astype(jnp.bfloat16)


def backward_chunks(place, grads, pre_blocks, w_in, w_out, sizes, shifts, split=False, waits=()):
    experts, groups, cap_rows, hidden = pre_blocks.shape
    features = w_in.shape[0]
    rows = experts * cap_rows
    chunks = len(shifts)
    parts = 2 if split else 1

    def whole(shape):
        return pl.BlockSpec(shape, lambda i, p: (0,) * len(shape))

    def shared(shift):
        return pl.BlockSpec(
            (experts, 1, cap_rows, hidden),
            lambda i, p: (0, lax.rem(p[0] + shift, groups), 0, 0),
        )

    out_shapes = [jax.ShapeDtypeStruct((rows, hidden), jnp.bfloat16)] * (2 * chunks) + [
        jax.ShapeDtypeStruct((rows // parts, features), jnp.bfloat16)
    ] * (parts * chunks)
    outs, token = call(
        functools.partial(backward_kernel, sizes, split),
        out_shapes,
        [place, w_in, w_out, *grads] + [pre_blocks] * chunks,
        4 * chunks * rows * hidden * features,
        grid_spec=pltpu.PrefetchScalarGridSpec(
            num_scalar_prefetch=1,
            grid=(1,),
            in_specs=[whole(w_in.shape), whole(w_out.shape)]
            + [whole(g.shape) for g in grads]
            + [shared(s) for s in shifts]
            + [ANYWHERE] * len(waits),
            out_specs=[*[whole(o.shape) for o in out_shapes], IN_VMEM],
            scratch_shapes=[pltpu.VMEM((rows, hidden), jnp.float32)],
        ),
        waits=waits,
    )
    return outs[:chunks], outs[chunks : 2 * chunks], outs[2 * chunks :], token


def forward_chunks(rows_list, w_in, w_out, sizes, split=False, waits=()):
    features, hidden = w_in.shape
    rows = sum(sizes[0])
    parts = 2 if split else 1
    return call(
        functools.partial(forward_kernel, sizes, split),
        [jax.ShapeDtypeStruct((rows // parts, features), jnp.bfloat16)] * (parts * len(sizes)),
        [w_in, w_out, *rows_list],
        4 * len(sizes) * rows * hidden * features,
        scratch_shapes=[
            pltpu.VMEM((rows, hidden), jnp.float32),
            pltpu.VMEM((rows, hidden), jnp.bfloat16),
        ],
        waits=waits,
    )


def weight_grad_kernel(lefts, rights, *refs):
    out_ref = refs[-1]

    def cut(pieces, sizes):
        spans, at = [], 0
        for ref, size in zip(pieces, sizes):
            spans.append((at, at + size, ref))
            at += size
        return spans

    left_spans = cut(refs[: len(lefts)], lefts)
    right_spans = cut(refs[len(lefts) : -1], rights)
    total = None
    for start, end, left in left_spans:
        for first, last, right in right_spans:
            low, high = max(start, first), min(end, last)
            if low >= high:
                continue
            part = matmul(
                left[low - start : high - start, :],
                right[low - first : high - first, :],
                ((0,), (0,)),
            )
            total = part if total is None else total + part
    out_ref[...] = total.astype(jnp.bfloat16)


def weight_grad(lefts, rights, tile, waits=()):
    left_cols, right_cols = lefts[0].shape[1], rights[0].shape[1]
    rows = sum(a.shape[0] for a in lefts)
    outs, token = call(
        functools.partial(
            weight_grad_kernel, [a.shape[0] for a in lefts], [a.shape[0] for a in rights]
        ),
        [jax.ShapeDtypeStruct((left_cols, right_cols), jnp.bfloat16)],
        [*lefts, *rights],
        2 * rows * left_cols * right_cols,
        in_specs=[pl.BlockSpec((a.shape[0], tile), lambda i: (0, i)) for a in lefts]
        + [pl.BlockSpec(a.shape, lambda i: (0, 0)) for a in rights],
        out_specs=[pl.BlockSpec((tile, right_cols), lambda i: (i, 0))],
        grid=(left_cols // tile,),
        waits=waits,
    )
    return outs[0], token


def first_grad_kernel(rows_ref, own_ref, left_ref, out_ref):
    blocks, _, slots, tile = rows_ref.shape
    total = None
    for c, right in enumerate((own_ref, left_ref)):
        rows = rows_ref[:, c].reshape(blocks * slots, tile)
        part = matmul(rows, right[...], ((0,), (0,)))
        total = part if total is None else total + part
    out_ref[...] = total


def first_grad(rows, rights, tile, waits):
    blocks, chunks, slots, features = rows.shape
    hidden = rights[0].shape[1]
    outs, token = call(
        first_grad_kernel,
        [jax.ShapeDtypeStruct((features, hidden), jnp.float32)],
        [rows, *rights],
        2 * blocks * chunks * slots * features * hidden,
        in_specs=[pl.BlockSpec((blocks, chunks, slots, tile), lambda i: (0, 0, 0, i))]
        + [pl.BlockSpec(a.shape, lambda i: (0, 0)) for a in rights],
        out_specs=[pl.BlockSpec((tile, hidden), lambda i: (i, 0))],
        grid=(features // tile,),
        waits=waits,
    )
    return outs[0], token


def last_grad_kernel(first_ref, one_ref, two_ref, right_one_ref, right_two_ref, out_ref):
    total = first_ref[...] + matmul(one_ref[...], right_one_ref[...], ((0,), (0,)))
    total = total + matmul(two_ref[...], right_two_ref[...], ((0,), (0,)))
    out_ref[...] = total.astype(jnp.bfloat16)


def last_grad(first, lefts, rights, tile):
    features, hidden = first.shape
    rows = lefts[0].shape[0]
    place = pl.BlockSpec((tile, hidden), lambda i: (i, 0))
    return call(
        last_grad_kernel,
        [jax.ShapeDtypeStruct((features, hidden), jnp.bfloat16)],
        [first, *lefts, *rights],
        4 * rows * features * hidden,
        in_specs=[place]
        + [pl.BlockSpec((rows, tile), lambda i: (0, i))] * 2
        + [pl.BlockSpec((rows, hidden), lambda i: (0, 0))] * 2,
        out_specs=[place],
        grid=(features // tile,),
    )[0][0]


def add_kernel(into_ref, more_ref, out_ref):
    out_ref[...] = (
        into_ref[...].astype(jnp.float32) + more_ref[...].astype(jnp.float32)
    ).astype(jnp.bfloat16)


def add_half(into, more, which, waits=()):
    half, features = more.shape
    place = pl.BlockSpec((half, features), lambda i: (which, 0))
    outs, token = call(
        add_kernel,
        [jax.ShapeDtypeStruct(into.shape, into.dtype)],
        [into, more],
        more.size,
        in_specs=[place, pl.BlockSpec((half, features), lambda i: (0, 0))],
        out_specs=[place],
        grid=(1,),
        input_output_aliases={0: 0},
        waits=waits,
    )
    return outs[0], token


def sum_kernel(one_ref, two_ref, three_ref, out_ref):
    out_ref[...] = (
        one_ref[...].astype(jnp.float32)
        + two_ref[...].astype(jnp.float32)
        + three_ref[...].astype(jnp.float32)
    ).astype(jnp.bfloat16)


def sum_three(one, two, three, waits=()):
    outs, token = call(
        sum_kernel,
        [jax.ShapeDtypeStruct(one.shape, one.dtype)],
        [one, two, three],
        2 * one.size,
        waits=waits,
    )
    return outs[0], token


def sum_split_kernel(one_ref, two_ref, three_ref, both_ref, out_ref, own_ref, left_ref, sems):
    copies = [
        pltpu.make_async_copy(both_ref.at[:, 0], own_ref, sems.at[0]),
        pltpu.make_async_copy(both_ref.at[:, 1], left_ref, sems.at[1]),
    ]
    for copy in copies:
        copy.start()
    sum_kernel(one_ref, two_ref, three_ref, out_ref)
    for copy in copies:
        copy.wait()


def sum_and_split(one, two, three, both, waits):
    experts, _, slots, features = both.shape
    whole = pl.BlockSpec(one.shape, lambda i: (0, 0))
    outs, _ = call(
        sum_split_kernel,
        [jax.ShapeDtypeStruct(one.shape, one.dtype)]
        + [jax.ShapeDtypeStruct((experts, slots, features), both.dtype)] * 2,
        [one, two, three, both],
        2 * one.size,
        in_specs=[whole, whole, whole, ANYWHERE],
        out_specs=[whole, IN_VMEM, IN_VMEM],
        grid=(1,),
        scratch_shapes=[pltpu.SemaphoreType.DMA((2,))],
        waits=waits,
    )
    return [o.reshape(one.shape) for o in outs]


def forward_out_kernel(cap_rows, arrival_ref, gate_ref, route_ref, returned_ref, out_ref):
    total = None
    for k, t in enumerate(forward_targets(route_ref[...], cap_rows)):
        part = gate_ref[:, k : k + 1] * matmul(
            hits_of(t, returned_ref.shape[0]), returned_ref[...], ((1,), (0,))
        )
        total = part if total is None else total + part
    out_ref[...] = (arrival_ref[...].astype(jnp.float32) + total).astype(jnp.bfloat16)


def backward_out_kernel(
    cap_rows, saved_ref, gain_ref, cot_ref, route_ref, slot_ref, returned_ref, out_ref
):
    pick = sum(
        hits_of(t, returned_ref.shape[0]).astype(jnp.float32)
        for t in backward_targets(route_ref[...], slot_ref[...], cap_rows)
    ).astype(jnp.bfloat16)
    scaled = gain_ref[...] * matmul(pick, returned_ref[...], ((1,), (0,)))
    plain = saved_ref[...].astype(jnp.float32)
    recip = rms_scale(plain)
    cubed = recip * recip * recip
    out_ref[...] = (
        cot_ref[...].astype(jnp.float32)
        + recip * scaled
        - plain * cubed * jnp.mean(scaled * plain, axis=-1, keepdims=True)
    ).astype(jnp.bfloat16)


def body(
    fwd_handoff,
    saved_input,
    grad_handoff,
    gain,
    route_fwd,
    gate_fwd,
    route_bwd,
    slot_bwd,
    gate_bwd,
    w_in,
    w_out,
    saved_pre,
):
    groups = lax.axis_size("expert") // EXPERTS
    tok_rows, features = fwd_handoff.shape[1:]
    choices = route_fwd.shape[2]
    cap_rows = tok_rows * choices // EXPERTS
    all_rows = EXPERTS * cap_rows
    half = all_rows // 2
    mine = jnp.asarray(lax.axis_index("expert") % groups, jnp.int32).reshape(1)
    w_in_local = w_in[0]
    w_out_local = w_out[0]
    pre_blocks = saved_pre[0].reshape(EXPERTS, groups, cap_rows, -1)
    rows_shape = [jax.ShapeDtypeStruct((all_rows, features), jnp.bfloat16)]
    token_shape = [jax.ShapeDtypeStruct((tok_rows, features), jnp.bfloat16)]
    pick_flops = 2 * tok_rows * all_rows * features

    def send(values):
        return exchange(values.reshape(EXPERTS, -1, features), groups).reshape(-1, features)

    cotangent = shifted(grad_handoff, "section", -1)
    arrival = shifted(after(fwd_handoff, cotangent), "section", 1)[0]
    cotangent = cotangent[0]

    (tagged,), tagged_token = call(
        tagged_kernel,
        [jax.ShapeDtypeStruct((tok_rows, features + 128), jnp.bfloat16)],
        [saved_input[0], gain, route_bwd[0], slot_bwd[0]],
        0,
    )
    tagged_left = turned(tagged, groups, 1)

    (grad_rows,), _ = call(
        functools.partial(pick_grad_kernel, cap_rows),
        rows_shape,
        [cotangent, gate_bwd[0], route_bwd[0], slot_bwd[0]],
        2 * pick_flops,
        waits=[tagged_token],
    )
    (rows_fwd,), _ = call(
        functools.partial(pick_forward_kernel, cap_rows),
        rows_shape,
        [arrival, gain, route_fwd[0]],
        pick_flops,
        waits=[tagged_left],
    )

    whole, halves = (all_rows,), (half, half)
    grads = send(grad_rows)
    grads_left, grads_right = turned(grads, groups, 1), turned(grads, groups, -1)
    sent_fwd = send(after(rows_fwd, grads))
    hidden_0, pre_grad_0, back_0, token_0 = backward_chunks(
        mine, [grads], pre_blocks, w_in_local, w_out_local, [whole], (0,)
    )
    grads_left_top, grads_right_bottom, cut_token = cut_halves(grads_left, grads_right, [token_0])
    grads_top = turned(grads_left_top, groups, 1)
    grads_bottom = turned(grads_right_bottom, groups, -1)
    (rows_bwd,), rows_token = call(
        functools.partial(picked_rows_kernel, choices),
        [jax.ShapeDtypeStruct((EXPERTS, 2, cap_rows, features), jnp.bfloat16)],
        [tagged, tagged_left],
        2 * pick_flops,
        waits=[cut_token],
    )
    sent_rows = send(rows_bwd).reshape(rows_bwd.shape)
    left, right = turned(sent_fwd, groups, 1), turned(sent_fwd, groups, -1)

    hidden_1, pre_grad_1, back_1, token_1 = backward_chunks(
        mine,
        [grads_left, grads_right],
        pre_blocks,
        w_in_local,
        w_out_local,
        [whole] * 2,
        (groups - 1, 1),
        waits=[cut_token, rows_token],
    )
    left_top, right_bottom, cut_token = cut_halves(left, right, [token_1])
    opposite_top = turned(left_top, groups, 1)
    opposite_bottom = turned(right_bottom, groups, -1)
    hidden_2, pre_grad_2, back_2, token_2 = backward_chunks(
        mine,
        [grads_top, grads_bottom],
        pre_blocks,
        w_in_local,
        w_out_local,
        [halves],
        (2,),
        split=True,
        waits=[token_1, cut_token],
    )
    back_top = turned(back_2[0], groups, 1)
    back_bottom = turned(back_2[1], groups, -1)

    fwd_0, token_3 = forward_chunks([sent_fwd], w_in_local, w_out_local, [whole], waits=[token_2])
    grad_w_out, token_4 = weight_grad(
        [*hidden_0, *hidden_1, *hidden_2],
        [grads, grads_left, grads_right, grads_top, grads_bottom],
        256,
        waits=[token_2],
    )
    back_to_left, token_5 = add_half(back_1[1], back_top, 0, [token_3, token_4])
    back_to_right, token_6 = add_half(back_1[0], back_bottom, 1, [token_3, token_4])
    back_left = turned(back_to_left, groups, 1)
    back_right = turned(back_to_right, groups, -1)
    fwd_1, token_7 = forward_chunks(
        [left, right], w_in_local, w_out_local, [whole] * 2, waits=[token_5, token_6]
    )
    fwd_2, _ = forward_chunks(
        [opposite_top, opposite_bottom],
        w_in_local,
        w_out_local,
        [halves],
        split=True,
        waits=[token_7],
    )
    fwd_top = turned(fwd_2[0], groups, 1)
    fwd_bottom = turned(fwd_2[1], groups, -1)

    fwd_to_left, token_8 = add_half(fwd_1[1], fwd_top, 0)
    fwd_to_right, token_9 = add_half(fwd_1[0], fwd_bottom, 1)
    back_sum, _ = sum_three(back_0[0], back_left, back_right, [token_8, token_9])
    return_bwd = send(back_sum)
    fwd_left = turned(fwd_to_left, groups, 1)
    fwd_right = turned(fwd_to_right, groups, -1)
    first, token_10 = first_grad(
        sent_rows, [pre_grad_0[0], pre_grad_1[0]], 256, [token_8, token_9]
    )
    fwd_sum, own_rows, left_rows = sum_and_split(
        fwd_0[0], fwd_left, fwd_right, sent_rows, [token_10]
    )
    return_fwd = send(after(fwd_sum, return_bwd))

    right_rows = turned(own_rows, groups, -1)
    opposite_rows = turned(left_rows, groups, 1)
    grad_w_in = last_grad(
        first, [right_rows, opposite_rows], [pre_grad_1[1], pre_grad_2[0]], 256
    )

    section_out = call(
        functools.partial(forward_out_kernel, cap_rows),
        token_shape,
        [arrival, gate_fwd[0], route_fwd[0], return_fwd],
        2 * pick_flops,
    )[0][0]
    input_grad = call(
        functools.partial(backward_out_kernel, cap_rows),
        token_shape,
        [saved_input[0], gain, cotangent, route_bwd[0], slot_bwd[0], return_bwd],
        pick_flops,
    )[0][0]
    return (section_out[None], input_grad[None], grad_w_in[None], grad_w_out[None])


def solution(mesh):
    placed = (
        P("section", "expert", None),
        P("section", "expert", None),
        P("section", "expert", None),
        P("section", None),
        P("section", "expert", None),
        P("section", "expert", None),
        P("section", "expert", None),
        P("section", "expert", None),
        P("section", "expert", None),
        P("section", None, "expert"),
        P("section", "expert", None),
        P("section", "expert", None),
    )
    return jax.shard_map(
        body,
        mesh=mesh,
        in_specs=placed,
        out_specs=(
            P("section", "expert", None),
            P("section", "expert", None),
            P("section", None, "expert"),
            P("section", "expert", None),
        ),
        check_vma=False,
    )
```

```python
import functools

import jax
import jax.numpy as jnp
from jax import lax
from jax.experimental import pallas as pl
from jax.experimental.pallas import tpu as pltpu
from jax.sharding import PartitionSpec as P

EXPERTS = 8


EPSILON = 1e-06
TANH_SCALE = 0.7978845608028654
CUBIC_COEF = 0.044715


def shifted(block, axis, distance):
    devices = range(lax.axis_size(axis))
    route = [((i - distance) % len(devices), i) for i in devices]
    return lax.ppermute(block, axis, route)


def turned(block, groups, distance):
    route = [
        (e * groups + g, e * groups + (g + distance) % groups)
        for e in range(EXPERTS)
        for g in range(groups)
    ]
    return lax.ppermute(block, "expert", route)


def exchange(block, groups):
    index_groups = [[e * groups + g for e in range(EXPERTS)] for g in range(groups)]
    return lax.all_to_all(
        block, "expert", split_axis=0, concat_axis=0, tiled=True, axis_index_groups=index_groups
    )


def after(value, *earlier):
    return lax.optimization_barrier((value, *earlier))[0]


def after(value, *earlier):
    return lax.optimization_barrier((value, *earlier))[0]


VMEM_BYTES = 30 * 1024 * 1024


def matmul(left, right, dims):
    return lax.dot_general(left, right, (dims, ((), ())), preferred_element_type=jnp.float32)


def call(kernel, out_shapes, operands, flops, in_specs=None, out_specs=None, **more):
    moved = sum(a.size * a.dtype.itemsize for a in operands)
    moved += sum(o.size * o.dtype.itemsize for o in out_shapes)
    if in_specs is None and "grid_spec" not in more:

        def whole(array):
            return pl.BlockSpec(array.shape, lambda i: (0,) * len(array.shape))

        more["grid"] = (1,)
        more["in_specs"] = [whole(a) for a in operands]
        more["out_specs"] = [whole(o) for o in out_shapes]
    elif in_specs is not None:
        more["in_specs"] = in_specs
        more["out_specs"] = out_specs
    return pl.pallas_call(
        kernel,
        out_shape=out_shapes,
        cost_estimate=pl.CostEstimate(flops=flops, bytes_accessed=moved, transcendentals=0),
        compiler_params=pltpu.CompilerParams(vmem_limit_bytes=VMEM_BYTES),
        **more,
    )(*operands)


def rms_scale(widened):
    return lax.rsqrt(jnp.mean(widened * widened, axis=-1, keepdims=True) + EPSILON)


def normed_of(tokens_ref, gain_ref):
    widened = tokens_ref[...].astype(jnp.float32)
    return (widened * rms_scale(widened) * gain_ref[...]).astype(jnp.bfloat16)


def hits_of(target, rows):
    ids = lax.broadcasted_iota(jnp.int32, (target.shape[0], rows), 1)
    return (target == ids).astype(jnp.float32).astype(jnp.bfloat16)


def forward_targets(route, cap_rows):
    tokens, choices = route.shape
    lanes = lax.broadcasted_iota(jnp.int32, (tokens, 128), 1)
    below = (
        lax.broadcasted_iota(jnp.int32, (tokens, tokens), 0)
        > lax.broadcasted_iota(jnp.int32, (tokens, tokens), 1)
    ).astype(jnp.float32)
    below = below.astype(jnp.bfloat16)
    ahead = jnp.zeros((1, 128), jnp.float32)
    targets = []
    for k in range(choices):
        expert = route[:, k : k + 1]
        named = (expert == lanes).astype(jnp.float32)
        count = matmul(below, named.astype(jnp.bfloat16), ((1,), (0,))) + ahead
        rank = jnp.sum(named * count, axis=1, keepdims=True).astype(jnp.int32)
        targets.append(expert * cap_rows + rank)
        ahead = ahead + jnp.sum(named, axis=0, keepdims=True)
    return targets


def backward_targets(route, slot, cap_rows):
    target = route * cap_rows + slot
    return [target[:, k : k + 1] for k in range(target.shape[1])]


def pick_forward_kernel(cap_rows, tokens_ref, gain_ref, route_ref, out_ref):
    normed = normed_of(tokens_ref, gain_ref)
    pick = sum(
        hits_of(t, out_ref.shape[0]).astype(jnp.float32)
        for t in forward_targets(route_ref[...], cap_rows)
    ).astype(jnp.bfloat16)
    out_ref[...] = matmul(pick, normed, ((0,), (0,))).astype(jnp.bfloat16)


def tagged_kernel(tokens_ref, gain_ref, route_ref, slot_ref, out_ref):
    tokens, features = tokens_ref.shape
    choices = route_ref.shape[1]
    out_ref[:, :features] = normed_of(tokens_ref, gain_ref)
    lanes = lax.broadcasted_iota(jnp.int32, (tokens, out_ref.shape[1] - features), 1)
    tags = jnp.zeros(lanes.shape, jnp.int32)
    for k in range(choices):
        tags = jnp.where(lanes == k, route_ref[:, k : k + 1], tags)
        tags = jnp.where(lanes == choices + k, slot_ref[:, k : k + 1], tags)
    out_ref[:, features:] = tags.astype(jnp.float32).astype(jnp.bfloat16)


def picked_rows_kernel(choices, own_ref, left_ref, right_ref, top_ref, bottom_ref, out_ref):
    experts, _, cap_rows, features = out_ref.shape
    for c, pieces in enumerate(((own_ref,), (left_ref,), (right_ref,), (top_ref, bottom_ref))):
        rows = None
        for ref in pieces:
            tags = ref[:, features:].astype(jnp.float32).astype(jnp.int32)
            pick = None
            for k in range(choices):
                target = tags[:, k : k + 1] * cap_rows + tags[:, choices + k : choices + k + 1]
                hit = hits_of(target, experts * cap_rows).astype(jnp.float32)
                pick = hit if pick is None else pick + hit
            part = matmul(pick.astype(jnp.bfloat16), ref[:, :features], ((0,), (0,)))
            rows = part if rows is None else rows + part
        out_ref[:, c] = rows.astype(jnp.bfloat16).reshape(experts, cap_rows, features)


def cut_kernel(left_ref, right_ref, top_ref, bottom_ref, sems):
    half = top_ref.shape[0]
    copies = [
        pltpu.make_async_copy(left_ref.at[:half], top_ref, sems.at[0]),
        pltpu.make_async_copy(right_ref.at[half:], bottom_ref, sems.at[1]),
    ]
    for copy in copies:
        copy.start()
    for copy in copies:
        copy.wait()


def cut_halves(left, right):
    anywhere = pl.BlockSpec(memory_space=pl.ANY)
    return call(
        cut_kernel,
        [jax.ShapeDtypeStruct((left.shape[0] // 2, left.shape[1]), left.dtype)] * 2,
        [left, right],
        0,
        in_specs=[anywhere] * 2,
        out_specs=[pl.BlockSpec(memory_space=pltpu.VMEM)] * 2,
        scratch_shapes=[pltpu.SemaphoreType.DMA((2,))],
    )


def pick_grad_kernel(cap_rows, cot_ref, gate_ref, route_ref, slot_ref, out_ref):
    cot = cot_ref[...].astype(jnp.float32)
    total = None
    for k, t in enumerate(backward_targets(route_ref[...], slot_ref[...], cap_rows)):
        gated = (gate_ref[:, k : k + 1] * cot).astype(jnp.bfloat16)
        part = matmul(hits_of(t, out_ref.shape[0]), gated, ((0,), (0,)))
        total = part if total is None else total + part
    out_ref[...] = total.astype(jnp.bfloat16)


def backward_kernel(sizes, split, place_ref, w_in_ref, w_out_ref, *refs):
    chunks = len(sizes)
    pieces = sum(len(s) for s in sizes)
    grads = list(refs[:pieces])
    pres = refs[pieces : pieces + chunks]
    outs = refs[pieces + chunks :]
    hidden_refs = outs[:chunks]
    pre_grad_refs = outs[chunks : 2 * chunks]
    back_refs = outs[2 * chunks : -1]
    wide = outs[-1]
    for c in range(chunks):
        row = 0
        for size in sizes[c]:
            wide[row : row + size, :] = matmul(grads.pop(0)[...], w_out_ref[...], ((1,), (1,)))
            row += size
        blocks, _, slots, _ = pres[c].shape
        for b in range(blocks):
            span = slice(b * slots, (b + 1) * slots)
            pre = pres[c][b, 0].astype(jnp.float32)
            square = pre * pre
            inner = TANH_SCALE * (pre + CUBIC_COEF * square * pre)
            tangent = jnp.tanh(inner)
            half = 0.5 * (1.0 + tangent)
            derivative = half + 0.5 * pre * (1.0 - tangent * tangent) * TANH_SCALE * (
                1.0 + 3.0 * CUBIC_COEF * square
            )
            hidden_refs[c][span, :] = (pre * half).astype(jnp.bfloat16)
            pre_grad_refs[c][span, :] = (wide[span, :] * derivative).astype(jnp.bfloat16)
        parts = 2 if split else 1
        for h in range(parts):
            span = slice(h * row // parts, (h + 1) * row // parts)
            back_refs[parts * c + h][...] = matmul(
                pre_grad_refs[c][span, :], w_in_ref[...], ((1,), (1,))
            ).astype(jnp.bfloat16)


def forward_kernel(sizes, split, w_in_ref, w_out_ref, *refs):
    chunks = len(sizes)
    pieces = sum(len(s) for s in sizes)
    rows = list(refs[:pieces])
    outs = refs[pieces:-2]
    wide, hidden = refs[-2:]
    for c in range(chunks):
        row = 0
        for size in sizes[c]:
            wide[row : row + size, :] = matmul(rows.pop(0)[...], w_in_ref[...], ((1,), (0,)))
            row += size
        for b in range(row // 32):
            span = slice(b * 32, (b + 1) * 32)
            pre = wide[span, :]
            tangent = jnp.tanh(TANH_SCALE * (pre + CUBIC_COEF * pre * pre * pre))
            hidden[span, :] = (0.5 * pre * (1.0 + tangent)).astype(jnp.bfloat16)
        parts = 2 if split else 1
        for h in range(parts):
            span = slice(h * row // parts, (h + 1) * row // parts)
            outs[parts * c + h][...] = matmul(
                hidden[span, :], w_out_ref[...], ((1,), (0,))
            ).astype(jnp.bfloat16)


def backward_chunks(place, grads, pre_blocks, w_in, w_out, sizes, shifts, split=False):
    experts, groups, cap_rows, hidden = pre_blocks.shape
    features = w_in.shape[0]
    rows = experts * cap_rows
    chunks = len(shifts)
    parts = 2 if split else 1

    def whole(shape):
        return pl.BlockSpec(shape, lambda i, p: (0,) * len(shape))

    def shared(shift):
        return pl.BlockSpec(
            (experts, 1, cap_rows, hidden),
            lambda i, p: (0, lax.rem(p[0] + shift, groups), 0, 0),
        )

    out_shapes = [jax.ShapeDtypeStruct((rows, hidden), jnp.bfloat16)] * (2 * chunks) + [
        jax.ShapeDtypeStruct((rows // parts, features), jnp.bfloat16)
    ] * (parts * chunks)
    outs = call(
        functools.partial(backward_kernel, sizes, split),
        out_shapes,
        [place, w_in, w_out, *grads] + [pre_blocks] * chunks,
        4 * chunks * rows * hidden * features,
        grid_spec=pltpu.PrefetchScalarGridSpec(
            num_scalar_prefetch=1,
            grid=(1,),
            in_specs=[whole(w_in.shape), whole(w_out.shape)]
            + [whole(g.shape) for g in grads]
            + [shared(s) for s in shifts],
            out_specs=[whole(o.shape) for o in out_shapes],
            scratch_shapes=[pltpu.VMEM((rows, hidden), jnp.float32)],
        ),
    )
    return outs[:chunks], outs[chunks : 2 * chunks], outs[2 * chunks :]


def forward_chunks(rows_list, w_in, w_out, sizes, split=False):
    features, hidden = w_in.shape
    rows = sum(sizes[0])
    parts = 2 if split else 1
    return call(
        functools.partial(forward_kernel, sizes, split),
        [jax.ShapeDtypeStruct((rows // parts, features), jnp.bfloat16)] * (parts * len(sizes)),
        [w_in, w_out, *rows_list],
        4 * len(sizes) * rows * hidden * features,
        scratch_shapes=[
            pltpu.VMEM((rows, hidden), jnp.float32),
            pltpu.VMEM((rows, hidden), jnp.bfloat16),
        ],
    )


def weight_grad_kernel(lefts, rights, *refs):
    out_ref = refs[-1]

    def cut(pieces, sizes):
        spans, at = [], 0
        for ref, size in zip(pieces, sizes):
            spans.append((at, at + size, ref))
            at += size
        return spans

    left_spans = cut(refs[: len(lefts)], lefts)
    right_spans = cut(refs[len(lefts) : -1], rights)
    total = None
    for start, end, left in left_spans:
        for first, last, right in right_spans:
            low, high = max(start, first), min(end, last)
            if low >= high:
                continue
            part = matmul(
                left[low - start : high - start, :],
                right[low - first : high - first, :],
                ((0,), (0,)),
            )
            total = part if total is None else total + part
    out_ref[...] = total.astype(jnp.bfloat16)


def weight_grad(lefts, rights, tile):
    left_cols, right_cols = lefts[0].shape[1], rights[0].shape[1]
    rows = sum(a.shape[0] for a in lefts)
    return call(
        functools.partial(
            weight_grad_kernel, [a.shape[0] for a in lefts], [a.shape[0] for a in rights]
        ),
        [jax.ShapeDtypeStruct((left_cols, right_cols), jnp.bfloat16)],
        [*lefts, *rights],
        2 * rows * left_cols * right_cols,
        in_specs=[pl.BlockSpec((a.shape[0], tile), lambda i: (0, i)) for a in lefts]
        + [pl.BlockSpec(a.shape, lambda i: (0, 0)) for a in rights],
        out_specs=[pl.BlockSpec((tile, right_cols), lambda i: (i, 0))],
        grid=(left_cols // tile,),
    )[0]


def exchanged_grad_kernel(rows_ref, *refs):
    out_ref = refs[-1]
    blocks, chunks, slots, tile = rows_ref.shape
    total = None
    for c in range(chunks):
        rows = rows_ref[:, c].reshape(blocks * slots, tile)
        part = matmul(rows, refs[c][...], ((0,), (0,)))
        total = part if total is None else total + part
    out_ref[...] = total.astype(jnp.bfloat16)


def exchanged_grad(rows, rights, tile):
    blocks, chunks, slots, features = rows.shape
    hidden = rights[0].shape[1]
    return call(
        exchanged_grad_kernel,
        [jax.ShapeDtypeStruct((features, hidden), jnp.bfloat16)],
        [rows, *rights],
        2 * blocks * chunks * slots * features * hidden,
        in_specs=[pl.BlockSpec((blocks, chunks, slots, tile), lambda i: (0, 0, 0, i))]
        + [pl.BlockSpec(a.shape, lambda i: (0, 0)) for a in rights],
        out_specs=[pl.BlockSpec((tile, hidden), lambda i: (i, 0))],
        grid=(features // tile,),
    )[0]


def add_kernel(into_ref, more_ref, out_ref):
    out_ref[...] = (
        into_ref[...].astype(jnp.float32) + more_ref[...].astype(jnp.float32)
    ).astype(jnp.bfloat16)


def add_half(into, more, which):
    half, features = more.shape
    place = pl.BlockSpec((half, features), lambda i: (which, 0))
    return call(
        add_kernel,
        [jax.ShapeDtypeStruct(into.shape, into.dtype)],
        [into, more],
        more.size,
        in_specs=[place, pl.BlockSpec((half, features), lambda i: (0, 0))],
        out_specs=[place],
        grid=(1,),
        input_output_aliases={0: 0},
    )[0]


def sum_kernel(one_ref, two_ref, three_ref, out_ref):
    out_ref[...] = (
        one_ref[...].astype(jnp.float32)
        + two_ref[...].astype(jnp.float32)
        + three_ref[...].astype(jnp.float32)
    ).astype(jnp.bfloat16)


def sum_three(one, two, three):
    return call(
        sum_kernel, [jax.ShapeDtypeStruct(one.shape, one.dtype)], [one, two, three], 2 * one.size
    )[0]


def forward_out_kernel(cap_rows, arrival_ref, gate_ref, route_ref, returned_ref, out_ref):
    total = None
    for k, t in enumerate(forward_targets(route_ref[...], cap_rows)):
        part = gate_ref[:, k : k + 1] * matmul(
            hits_of(t, returned_ref.shape[0]), returned_ref[...], ((1,), (0,))
        )
        total = part if total is None else total + part
    out_ref[...] = (arrival_ref[...].astype(jnp.float32) + total).astype(jnp.bfloat16)


def backward_out_kernel(
    cap_rows, saved_ref, gain_ref, cot_ref, route_ref, slot_ref, returned_ref, out_ref
):
    pick = sum(
        hits_of(t, returned_ref.shape[0]).astype(jnp.float32)
        for t in backward_targets(route_ref[...], slot_ref[...], cap_rows)
    ).astype(jnp.bfloat16)
    scaled = gain_ref[...] * matmul(pick, returned_ref[...], ((1,), (0,)))
    plain = saved_ref[...].astype(jnp.float32)
    recip = rms_scale(plain)
    cubed = recip * recip * recip
    out_ref[...] = (
        cot_ref[...].astype(jnp.float32)
        + recip * scaled
        - plain * cubed * jnp.mean(scaled * plain, axis=-1, keepdims=True)
    ).astype(jnp.bfloat16)


def body(
    fwd_handoff,
    saved_input,
    grad_handoff,
    gain,
    route_fwd,
    gate_fwd,
    route_bwd,
    slot_bwd,
    gate_bwd,
    w_in,
    w_out,
    saved_pre,
):
    groups = lax.axis_size("expert") // EXPERTS
    tok_rows, features = fwd_handoff.shape[1:]
    choices = route_fwd.shape[2]
    cap_rows = tok_rows * choices // EXPERTS
    all_rows = EXPERTS * cap_rows
    half = all_rows // 2
    mine = jnp.asarray(lax.axis_index("expert") % groups, jnp.int32).reshape(1)
    w_in_local = w_in[0]
    w_out_local = w_out[0]
    pre_blocks = saved_pre[0].reshape(EXPERTS, groups, cap_rows, -1)
    rows_shape = [jax.ShapeDtypeStruct((all_rows, features), jnp.bfloat16)]
    token_shape = [jax.ShapeDtypeStruct((tok_rows, features), jnp.bfloat16)]
    pick_flops = 2 * tok_rows * all_rows * features

    def send(values):
        return exchange(values.reshape(EXPERTS, -1, features), groups).reshape(-1, features)

    cotangent = shifted(grad_handoff, "section", -1)
    arrival = shifted(after(fwd_handoff, cotangent), "section", 1)[0]
    cotangent = cotangent[0]

    tagged = call(
        tagged_kernel,
        [jax.ShapeDtypeStruct((tok_rows, features + 128), jnp.bfloat16)],
        [saved_input[0], gain, route_bwd[0], slot_bwd[0]],
        0,
    )[0]
    tagged_left, tagged_right = turned(tagged, groups, 1), turned(tagged, groups, -1)
    tagged_left_top, tagged_right_bottom = cut_halves(tagged_left, tagged_right)
    tagged_top = turned(tagged_left_top, groups, 1)
    tagged_bottom = turned(tagged_right_bottom, groups, -1)

    grad_rows = call(
        functools.partial(pick_grad_kernel, cap_rows),
        rows_shape,
        [after(cotangent, tagged), gate_bwd[0], route_bwd[0], slot_bwd[0]],
        2 * pick_flops,
    )[0]
    rows_fwd = call(
        functools.partial(pick_forward_kernel, cap_rows),
        rows_shape,
        [after(arrival, tagged_left_top, tagged_right_bottom), gain, route_fwd[0]],
        pick_flops,
    )[0]

    grads = send(grad_rows)
    grads_left, grads_right = turned(grads, groups, 1), turned(grads, groups, -1)
    sent_fwd = send(after(rows_fwd, grads))
    whole, halves = (all_rows,), (half, half)
    hidden_0, pre_grad_0, back_0 = backward_chunks(
        mine, [grads], pre_blocks, w_in_local, w_out_local, [whole], (0,)
    )
    rows_bwd = call(
        functools.partial(picked_rows_kernel, choices),
        [jax.ShapeDtypeStruct((EXPERTS, groups, cap_rows, features), jnp.bfloat16)],
        [after(tagged, rows_fwd, *back_0), tagged_left, tagged_right, tagged_top, tagged_bottom],
        groups * pick_flops,
    )[0]
    grads_left_top, grads_right_bottom = cut_halves(after(grads_left, rows_bwd), grads_right)
    grads_top = turned(grads_left_top, groups, 1)
    grads_bottom = turned(grads_right_bottom, groups, -1)
    ready = after(sent_fwd, grads_left, grads_right)
    left, right = turned(ready, groups, 1), turned(ready, groups, -1)
    sent_rows = send(after(rows_bwd, sent_fwd, grads_left_top, grads_right_bottom))

    hidden_1, pre_grad_1, back_1 = backward_chunks(
        mine,
        [after(grads_left, sent_fwd), grads_right],
        pre_blocks,
        w_in_local,
        w_out_local,
        [whole] * 2,
        (groups - 1, 1),
    )
    hidden_2, pre_grad_2, back_2 = backward_chunks(
        mine,
        [after(grads_top, *back_1), grads_bottom],
        pre_blocks,
        w_in_local,
        w_out_local,
        [halves],
        (2,),
        split=True,
    )
    back_top = turned(back_2[0], groups, 1)
    back_bottom = turned(back_2[1], groups, -1)

    left_top, right_bottom = cut_halves(left, right)
    opposite_top = turned(left_top, groups, 1)
    opposite_bottom = turned(right_bottom, groups, -1)
    grad_w_out = weight_grad(
        [*hidden_0, *hidden_1, *hidden_2],
        [after(grads, left_top, right_bottom), grads_left, grads_right, grads_top, grads_bottom],
        256,
    )
    fwd_0 = forward_chunks([after(sent_fwd, left_top, right_bottom)], w_in_local, w_out_local, [whole])

    arrived = (grad_w_out, *fwd_0, opposite_top, opposite_bottom)
    back_to_left = add_half(back_1[1], after(back_top, *arrived), 0)
    back_to_right = add_half(back_1[0], after(back_bottom, *arrived), 1)
    back_left = turned(back_to_left, groups, 1)
    back_right = turned(back_to_right, groups, -1)
    fwd_1 = forward_chunks(
        [after(left, back_to_left, back_to_right), right], w_in_local, w_out_local, [whole] * 2
    )
    fwd_2 = forward_chunks(
        [after(opposite_top, *fwd_1), opposite_bottom], w_in_local, w_out_local, [halves], split=True
    )
    fwd_top = turned(fwd_2[0], groups, 1)
    fwd_bottom = turned(fwd_2[1], groups, -1)

    back_sum = sum_three(after(back_0[0], *fwd_2), back_left, back_right)
    fwd_to_left = add_half(fwd_1[1], fwd_top, 0)
    fwd_to_right = add_half(fwd_1[0], fwd_bottom, 1)
    return_bwd = send(after(back_sum, sent_rows, fwd_to_left, fwd_to_right))
    grad_w_in = exchanged_grad(
        sent_rows.reshape(rows_bwd.shape), [*pre_grad_0, *pre_grad_1, *pre_grad_2], 256
    )

    fwd_left = turned(fwd_to_left, groups, 1)
    fwd_right = turned(fwd_to_right, groups, -1)
    fwd_sum = sum_three(fwd_0[0], after(fwd_left, grad_w_in), fwd_right)
    return_fwd = send(after(fwd_sum, return_bwd))

    section_out = call(
        functools.partial(forward_out_kernel, cap_rows),
        token_shape,
        [arrival, gate_fwd[0], route_fwd[0], return_fwd],
        2 * pick_flops,
    )[0]
    input_grad = call(
        functools.partial(backward_out_kernel, cap_rows),
        token_shape,
        [saved_input[0], gain, cotangent, route_bwd[0], slot_bwd[0], return_bwd],
        pick_flops,
    )[0]
    return (section_out[None], input_grad[None], grad_w_in[None], grad_w_out[None])


def solution(mesh):
    placed = (
        P("section", "expert", None),
        P("section", "expert", None),
        P("section", "expert", None),
        P("section", None),
        P("section", "expert", None),
        P("section", "expert", None),
        P("section", "expert", None),
        P("section", "expert", None),
        P("section", "expert", None),
        P("section", None, "expert"),
        P("section", "expert", None),
        P("section", "expert", None),
    )
    return jax.shard_map(
        body,
        mesh=mesh,
        in_specs=placed,
        out_specs=(
            P("section", "expert", None),
            P("section", "expert", None),
            P("section", None, "expert"),
            P("section", "expert", None),
        ),
        check_vma=False,
    )
```

```python
import functools

import jax
import jax.numpy as jnp
from jax import lax
from jax.experimental import pallas as pl
from jax.experimental.pallas import tpu as pltpu
from jax.sharding import PartitionSpec as P

EXPERTS = 8


EPSILON = 1e-06
TANH_SCALE = 0.7978845608028654
CUBIC_COEF = 0.044715


def shifted(block, axis, distance):
    devices = range(lax.axis_size(axis))
    route = [((i - distance) % len(devices), i) for i in devices]
    return lax.ppermute(block, axis, route)


def turned(block, groups, distance):
    route = [
        (e * groups + g, e * groups + (g + distance) % groups)
        for e in range(EXPERTS)
        for g in range(groups)
    ]
    return lax.ppermute(block, "expert", route)


def exchange(block, groups):
    index_groups = [[e * groups + g for e in range(EXPERTS)] for g in range(groups)]
    return lax.all_to_all(
        block, "expert", split_axis=0, concat_axis=0, tiled=True, axis_index_groups=index_groups
    )


def after(value, *earlier):
    return lax.optimization_barrier((value, *earlier))[0]


def after(value, *earlier):
    return lax.optimization_barrier((value, *earlier))[0]


VMEM_BYTES = 30 * 1024 * 1024


def matmul(left, right, dims):
    return lax.dot_general(left, right, (dims, ((), ())), preferred_element_type=jnp.float32)


def call(kernel, out_shapes, operands, flops, in_specs=None, out_specs=None, **more):
    moved = sum(a.size * a.dtype.itemsize for a in operands)
    moved += sum(o.size * o.dtype.itemsize for o in out_shapes)
    if in_specs is None and "grid_spec" not in more:

        def whole(array):
            return pl.BlockSpec(array.shape, lambda i: (0,) * len(array.shape))

        more["grid"] = (1,)
        more["in_specs"] = [whole(a) for a in operands]
        more["out_specs"] = [whole(o) for o in out_shapes]
    elif in_specs is not None:
        more["in_specs"] = in_specs
        more["out_specs"] = out_specs
    return pl.pallas_call(
        kernel,
        out_shape=out_shapes,
        cost_estimate=pl.CostEstimate(flops=flops, bytes_accessed=moved, transcendentals=0),
        compiler_params=pltpu.CompilerParams(vmem_limit_bytes=VMEM_BYTES),
        **more,
    )(*operands)


def rms_scale(widened):
    return lax.rsqrt(jnp.mean(widened * widened, axis=-1, keepdims=True) + EPSILON)


def normed_of(tokens_ref, gain_ref):
    widened = tokens_ref[...].astype(jnp.float32)
    return (widened * rms_scale(widened) * gain_ref[...]).astype(jnp.bfloat16)


def hits_of(target, rows):
    ids = lax.broadcasted_iota(jnp.int32, (target.shape[0], rows), 1)
    return (target == ids).astype(jnp.float32).astype(jnp.bfloat16)


def forward_targets(route, cap_rows):
    tokens, choices = route.shape
    lanes = lax.broadcasted_iota(jnp.int32, (tokens, 128), 1)
    below = (
        lax.broadcasted_iota(jnp.int32, (tokens, tokens), 0)
        > lax.broadcasted_iota(jnp.int32, (tokens, tokens), 1)
    ).astype(jnp.float32)
    below = below.astype(jnp.bfloat16)
    ahead = jnp.zeros((1, 128), jnp.float32)
    targets = []
    for k in range(choices):
        expert = route[:, k : k + 1]
        named = (expert == lanes).astype(jnp.float32)
        count = matmul(below, named.astype(jnp.bfloat16), ((1,), (0,))) + ahead
        rank = jnp.sum(named * count, axis=1, keepdims=True).astype(jnp.int32)
        targets.append(expert * cap_rows + rank)
        ahead = ahead + jnp.sum(named, axis=0, keepdims=True)
    return targets


def backward_targets(route, slot, cap_rows):
    target = route * cap_rows + slot
    return [target[:, k : k + 1] for k in range(target.shape[1])]


def pick_forward_kernel(cap_rows, tokens_ref, gain_ref, route_ref, out_ref):
    normed = normed_of(tokens_ref, gain_ref)
    pick = sum(
        hits_of(t, out_ref.shape[0]).astype(jnp.float32)
        for t in forward_targets(route_ref[...], cap_rows)
    ).astype(jnp.bfloat16)
    out_ref[...] = matmul(pick, normed, ((0,), (0,))).astype(jnp.bfloat16)


def tagged_kernel(tokens_ref, gain_ref, route_ref, slot_ref, out_ref):
    tokens, features = tokens_ref.shape
    choices = route_ref.shape[1]
    out_ref[:, :features] = normed_of(tokens_ref, gain_ref)
    lanes = lax.broadcasted_iota(jnp.int32, (tokens, out_ref.shape[1] - features), 1)
    tags = jnp.zeros(lanes.shape, jnp.int32)
    for k in range(choices):
        tags = jnp.where(lanes == k, route_ref[:, k : k + 1], tags)
        tags = jnp.where(lanes == choices + k, slot_ref[:, k : k + 1], tags)
    out_ref[:, features:] = tags.astype(jnp.float32).astype(jnp.bfloat16)


def picked_rows_kernel(choices, own_ref, left_ref, right_ref, top_ref, bottom_ref, out_ref):
    experts, _, cap_rows, features = out_ref.shape
    for c, pieces in enumerate(((own_ref,), (left_ref,), (right_ref,), (top_ref, bottom_ref))):
        rows = None
        for ref in pieces:
            tags = ref[:, features:].astype(jnp.float32).astype(jnp.int32)
            pick = None
            for k in range(choices):
                target = tags[:, k : k + 1] * cap_rows + tags[:, choices + k : choices + k + 1]
                hit = hits_of(target, experts * cap_rows).astype(jnp.float32)
                pick = hit if pick is None else pick + hit
            part = matmul(pick.astype(jnp.bfloat16), ref[:, :features], ((0,), (0,)))
            rows = part if rows is None else rows + part
        out_ref[:, c] = rows.astype(jnp.bfloat16).reshape(experts, cap_rows, features)


def cut_kernel(left_ref, right_ref, top_ref, bottom_ref, sems):
    half = top_ref.shape[0]
    copies = [
        pltpu.make_async_copy(left_ref.at[:half], top_ref, sems.at[0]),
        pltpu.make_async_copy(right_ref.at[half:], bottom_ref, sems.at[1]),
    ]
    for copy in copies:
        copy.start()
    for copy in copies:
        copy.wait()


def cut_halves(left, right):
    anywhere = pl.BlockSpec(memory_space=pl.ANY)
    return call(
        cut_kernel,
        [jax.ShapeDtypeStruct((left.shape[0] // 2, left.shape[1]), left.dtype)] * 2,
        [left, right],
        0,
        in_specs=[anywhere] * 2,
        out_specs=[pl.BlockSpec(memory_space=pltpu.VMEM)] * 2,
        scratch_shapes=[pltpu.SemaphoreType.DMA((2,))],
    )


def pick_grad_kernel(cap_rows, cot_ref, gate_ref, route_ref, slot_ref, out_ref):
    cot = cot_ref[...].astype(jnp.float32)
    total = None
    for k, t in enumerate(backward_targets(route_ref[...], slot_ref[...], cap_rows)):
        gated = (gate_ref[:, k : k + 1] * cot).astype(jnp.bfloat16)
        part = matmul(hits_of(t, out_ref.shape[0]), gated, ((0,), (0,)))
        total = part if total is None else total + part
    out_ref[...] = total.astype(jnp.bfloat16)


def backward_kernel(sizes, split, place_ref, w_in_ref, w_out_ref, *refs):
    chunks = len(sizes)
    pieces = sum(len(s) for s in sizes)
    grads = list(refs[:pieces])
    pres = refs[pieces : pieces + chunks]
    outs = refs[pieces + chunks :]
    hidden_refs = outs[:chunks]
    pre_grad_refs = outs[chunks : 2 * chunks]
    back_refs = outs[2 * chunks : -1]
    wide = outs[-1]
    for c in range(chunks):
        row = 0
        for size in sizes[c]:
            wide[row : row + size, :] = matmul(grads.pop(0)[...], w_out_ref[...], ((1,), (1,)))
            row += size
        blocks, _, slots, _ = pres[c].shape
        for b in range(blocks):
            span = slice(b * slots, (b + 1) * slots)
            pre = pres[c][b, 0].astype(jnp.float32)
            square = pre * pre
            inner = TANH_SCALE * (pre + CUBIC_COEF * square * pre)
            tangent = jnp.tanh(inner)
            half = 0.5 * (1.0 + tangent)
            derivative = half + 0.5 * pre * (1.0 - tangent * tangent) * TANH_SCALE * (
                1.0 + 3.0 * CUBIC_COEF * square
            )
            hidden_refs[c][span, :] = (pre * half).astype(jnp.bfloat16)
            pre_grad_refs[c][span, :] = (wide[span, :] * derivative).astype(jnp.bfloat16)
        parts = 2 if split else 1
        for h in range(parts):
            span = slice(h * row // parts, (h + 1) * row // parts)
            back_refs[parts * c + h][...] = matmul(
                pre_grad_refs[c][span, :], w_in_ref[...], ((1,), (1,))
            ).astype(jnp.bfloat16)


def forward_kernel(sizes, split, w_in_ref, w_out_ref, *refs):
    chunks = len(sizes)
    pieces = sum(len(s) for s in sizes)
    rows = list(refs[:pieces])
    outs = refs[pieces:-2]
    wide, hidden = refs[-2:]
    for c in range(chunks):
        row = 0
        for size in sizes[c]:
            wide[row : row + size, :] = matmul(rows.pop(0)[...], w_in_ref[...], ((1,), (0,)))
            row += size
        for b in range(row // 32):
            span = slice(b * 32, (b + 1) * 32)
            pre = wide[span, :]
            tangent = jnp.tanh(TANH_SCALE * (pre + CUBIC_COEF * pre * pre * pre))
            hidden[span, :] = (0.5 * pre * (1.0 + tangent)).astype(jnp.bfloat16)
        parts = 2 if split else 1
        for h in range(parts):
            span = slice(h * row // parts, (h + 1) * row // parts)
            outs[parts * c + h][...] = matmul(
                hidden[span, :], w_out_ref[...], ((1,), (0,))
            ).astype(jnp.bfloat16)


def backward_chunks(place, grads, pre_blocks, w_in, w_out, sizes, shifts, split=False):
    experts, groups, cap_rows, hidden = pre_blocks.shape
    features = w_in.shape[0]
    rows = experts * cap_rows
    chunks = len(shifts)
    parts = 2 if split else 1

    def whole(shape):
        return pl.BlockSpec(shape, lambda i, p: (0,) * len(shape))

    def shared(shift):
        return pl.BlockSpec(
            (experts, 1, cap_rows, hidden),
            lambda i, p: (0, lax.rem(p[0] + shift, groups), 0, 0),
        )

    out_shapes = [jax.ShapeDtypeStruct((rows, hidden), jnp.bfloat16)] * (2 * chunks) + [
        jax.ShapeDtypeStruct((rows // parts, features), jnp.bfloat16)
    ] * (parts * chunks)
    outs = call(
        functools.partial(backward_kernel, sizes, split),
        out_shapes,
        [place, w_in, w_out, *grads] + [pre_blocks] * chunks,
        4 * chunks * rows * hidden * features,
        grid_spec=pltpu.PrefetchScalarGridSpec(
            num_scalar_prefetch=1,
            grid=(1,),
            in_specs=[whole(w_in.shape), whole(w_out.shape)]
            + [whole(g.shape) for g in grads]
            + [shared(s) for s in shifts],
            out_specs=[whole(o.shape) for o in out_shapes],
            scratch_shapes=[pltpu.VMEM((rows, hidden), jnp.float32)],
        ),
    )
    return outs[:chunks], outs[chunks : 2 * chunks], outs[2 * chunks :]


def forward_chunks(rows_list, w_in, w_out, sizes, split=False):
    features, hidden = w_in.shape
    rows = sum(sizes[0])
    parts = 2 if split else 1
    return call(
        functools.partial(forward_kernel, sizes, split),
        [jax.ShapeDtypeStruct((rows // parts, features), jnp.bfloat16)] * (parts * len(sizes)),
        [w_in, w_out, *rows_list],
        4 * len(sizes) * rows * hidden * features,
        scratch_shapes=[
            pltpu.VMEM((rows, hidden), jnp.float32),
            pltpu.VMEM((rows, hidden), jnp.bfloat16),
        ],
    )


def weight_grad_kernel(lefts, rights, *refs):
    out_ref = refs[-1]

    def cut(pieces, sizes):
        spans, at = [], 0
        for ref, size in zip(pieces, sizes):
            spans.append((at, at + size, ref))
            at += size
        return spans

    left_spans = cut(refs[: len(lefts)], lefts)
    right_spans = cut(refs[len(lefts) : -1], rights)
    total = None
    for start, end, left in left_spans:
        for first, last, right in right_spans:
            low, high = max(start, first), min(end, last)
            if low >= high:
                continue
            part = matmul(
                left[low - start : high - start, :],
                right[low - first : high - first, :],
                ((0,), (0,)),
            )
            total = part if total is None else total + part
    out_ref[...] = total.astype(jnp.bfloat16)


def weight_grad(lefts, rights, tile):
    left_cols, right_cols = lefts[0].shape[1], rights[0].shape[1]
    rows = sum(a.shape[0] for a in lefts)
    return call(
        functools.partial(
            weight_grad_kernel, [a.shape[0] for a in lefts], [a.shape[0] for a in rights]
        ),
        [jax.ShapeDtypeStruct((left_cols, right_cols), jnp.bfloat16)],
        [*lefts, *rights],
        2 * rows * left_cols * right_cols,
        in_specs=[pl.BlockSpec((a.shape[0], tile), lambda i: (0, i)) for a in lefts]
        + [pl.BlockSpec(a.shape, lambda i: (0, 0)) for a in rights],
        out_specs=[pl.BlockSpec((tile, right_cols), lambda i: (i, 0))],
        grid=(left_cols // tile,),
    )[0]


def exchanged_grad_kernel(rows_ref, *refs):
    out_ref = refs[-1]
    blocks, chunks, slots, tile = rows_ref.shape
    total = None
    for c in range(chunks):
        rows = rows_ref[:, c].reshape(blocks * slots, tile)
        part = matmul(rows, refs[c][...], ((0,), (0,)))
        total = part if total is None else total + part
    out_ref[...] = total.astype(jnp.bfloat16)


def exchanged_grad(rows, rights, tile):
    blocks, chunks, slots, features = rows.shape
    hidden = rights[0].shape[1]
    return call(
        exchanged_grad_kernel,
        [jax.ShapeDtypeStruct((features, hidden), jnp.bfloat16)],
        [rows, *rights],
        2 * blocks * chunks * slots * features * hidden,
        in_specs=[pl.BlockSpec((blocks, chunks, slots, tile), lambda i: (0, 0, 0, i))]
        + [pl.BlockSpec(a.shape, lambda i: (0, 0)) for a in rights],
        out_specs=[pl.BlockSpec((tile, hidden), lambda i: (i, 0))],
        grid=(features // tile,),
    )[0]


def add_kernel(into_ref, more_ref, out_ref):
    out_ref[...] = (
        into_ref[...].astype(jnp.float32) + more_ref[...].astype(jnp.float32)
    ).astype(jnp.bfloat16)


def add_half(into, more, which):
    half, features = more.shape
    place = pl.BlockSpec((half, features), lambda i: (which, 0))
    return call(
        add_kernel,
        [jax.ShapeDtypeStruct(into.shape, into.dtype)],
        [into, more],
        more.size,
        in_specs=[place, pl.BlockSpec((half, features), lambda i: (0, 0))],
        out_specs=[place],
        grid=(1,),
        input_output_aliases={0: 0},
    )[0]


def sum_kernel(one_ref, two_ref, three_ref, out_ref):
    out_ref[...] = (
        one_ref[...].astype(jnp.float32)
        + two_ref[...].astype(jnp.float32)
        + three_ref[...].astype(jnp.float32)
    ).astype(jnp.bfloat16)


def sum_three(one, two, three):
    return call(
        sum_kernel, [jax.ShapeDtypeStruct(one.shape, one.dtype)], [one, two, three], 2 * one.size
    )[0]


def forward_out_kernel(cap_rows, arrival_ref, gate_ref, route_ref, returned_ref, out_ref):
    total = None
    for k, t in enumerate(forward_targets(route_ref[...], cap_rows)):
        part = gate_ref[:, k : k + 1] * matmul(
            hits_of(t, returned_ref.shape[0]), returned_ref[...], ((1,), (0,))
        )
        total = part if total is None else total + part
    out_ref[...] = (arrival_ref[...].astype(jnp.float32) + total).astype(jnp.bfloat16)


def backward_out_kernel(
    cap_rows, saved_ref, gain_ref, cot_ref, route_ref, slot_ref, returned_ref, out_ref
):
    pick = sum(
        hits_of(t, returned_ref.shape[0]).astype(jnp.float32)
        for t in backward_targets(route_ref[...], slot_ref[...], cap_rows)
    ).astype(jnp.bfloat16)
    scaled = gain_ref[...] * matmul(pick, returned_ref[...], ((1,), (0,)))
    plain = saved_ref[...].astype(jnp.float32)
    recip = rms_scale(plain)
    cubed = recip * recip * recip
    out_ref[...] = (
        cot_ref[...].astype(jnp.float32)
        + recip * scaled
        - plain * cubed * jnp.mean(scaled * plain, axis=-1, keepdims=True)
    ).astype(jnp.bfloat16)


def body(
    fwd_handoff,
    saved_input,
    grad_handoff,
    gain,
    route_fwd,
    gate_fwd,
    route_bwd,
    slot_bwd,
    gate_bwd,
    w_in,
    w_out,
    saved_pre,
):
    groups = lax.axis_size("expert") // EXPERTS
    tok_rows, features = fwd_handoff.shape[1:]
    choices = route_fwd.shape[2]
    cap_rows = tok_rows * choices // EXPERTS
    all_rows = EXPERTS * cap_rows
    half = all_rows // 2
    mine = jnp.asarray(lax.axis_index("expert") % groups, jnp.int32).reshape(1)
    w_in_local = w_in[0]
    w_out_local = w_out[0]
    pre_blocks = saved_pre[0].reshape(EXPERTS, groups, cap_rows, -1)
    rows_shape = [jax.ShapeDtypeStruct((all_rows, features), jnp.bfloat16)]
    token_shape = [jax.ShapeDtypeStruct((tok_rows, features), jnp.bfloat16)]
    pick_flops = 2 * tok_rows * all_rows * features

    def send(values):
        return exchange(values.reshape(EXPERTS, -1, features), groups).reshape(-1, features)

    cotangent = shifted(grad_handoff, "section", -1)
    arrival = shifted(after(fwd_handoff, cotangent), "section", 1)[0]
    cotangent = cotangent[0]

    tagged = call(
        tagged_kernel,
        [jax.ShapeDtypeStruct((tok_rows, features + 128), jnp.bfloat16)],
        [saved_input[0], gain, route_bwd[0], slot_bwd[0]],
        0,
    )[0]
    tagged_left, tagged_right = turned(tagged, groups, 1), turned(tagged, groups, -1)
    tagged_left_top, tagged_right_bottom = cut_halves(tagged_left, tagged_right)
    tagged_top = turned(tagged_left_top, groups, 1)
    tagged_bottom = turned(tagged_right_bottom, groups, -1)

    grad_rows = call(
        functools.partial(pick_grad_kernel, cap_rows),
        rows_shape,
        [after(cotangent, tagged), gate_bwd[0], route_bwd[0], slot_bwd[0]],
        2 * pick_flops,
    )[0]
    rows_fwd = call(
        functools.partial(pick_forward_kernel, cap_rows),
        rows_shape,
        [after(arrival, tagged_top, tagged_bottom), gain, route_fwd[0]],
        pick_flops,
    )[0]

    grads = send(grad_rows)
    grads_left, grads_right = turned(grads, groups, 1), turned(grads, groups, -1)
    sent_fwd = send(after(rows_fwd, grads))
    whole, halves = (all_rows,), (half, half)
    hidden_0, pre_grad_0, back_0 = backward_chunks(
        mine, [grads], pre_blocks, w_in_local, w_out_local, [whole], (0,)
    )
    rows_bwd = call(
        functools.partial(picked_rows_kernel, choices),
        [jax.ShapeDtypeStruct((EXPERTS, groups, cap_rows, features), jnp.bfloat16)],
        [after(tagged, rows_fwd, *back_0), tagged_left, tagged_right, tagged_top, tagged_bottom],
        groups * pick_flops,
    )[0]
    grads_left_top, grads_right_bottom = cut_halves(after(grads_left, rows_bwd), grads_right)
    grads_top = turned(grads_left_top, groups, 1)
    grads_bottom = turned(grads_right_bottom, groups, -1)
    ready = after(sent_fwd, grads_left, grads_right)
    left, right = turned(ready, groups, 1), turned(ready, groups, -1)
    sent_rows = send(after(rows_bwd, sent_fwd, grads_left_top, grads_right_bottom))

    hidden_1, pre_grad_1, back_1 = backward_chunks(
        mine,
        [after(grads_left, sent_fwd), grads_right],
        pre_blocks,
        w_in_local,
        w_out_local,
        [whole] * 2,
        (groups - 1, 1),
    )
    hidden_2, pre_grad_2, back_2 = backward_chunks(
        mine,
        [after(grads_top, *back_1), grads_bottom],
        pre_blocks,
        w_in_local,
        w_out_local,
        [halves],
        (2,),
        split=True,
    )
    back_top = turned(back_2[0], groups, 1)
    back_bottom = turned(back_2[1], groups, -1)

    left_top, right_bottom = cut_halves(left, right)
    opposite_top = turned(left_top, groups, 1)
    opposite_bottom = turned(right_bottom, groups, -1)
    fwd_0 = forward_chunks([after(sent_fwd, left_top, right_bottom)], w_in_local, w_out_local, [whole])

    arrived = tuple(fwd_0)
    back_to_left = add_half(back_1[1], after(back_top, *arrived), 0)
    back_to_right = add_half(back_1[0], after(back_bottom, *arrived), 1)
    back_left = turned(back_to_left, groups, 1)
    back_right = turned(back_to_right, groups, -1)
    fwd_1 = forward_chunks(
        [after(left, back_to_left, back_to_right), right], w_in_local, w_out_local, [whole] * 2
    )
    fwd_2 = forward_chunks(
        [after(opposite_top, *fwd_1), opposite_bottom], w_in_local, w_out_local, [halves], split=True
    )
    grad_w_out = weight_grad(
        [*hidden_0, *hidden_1, *hidden_2],
        [after(grads, *fwd_2), grads_left, grads_right, grads_top, grads_bottom],
        256,
    )
    fwd_top = turned(fwd_2[0], groups, 1)
    fwd_bottom = turned(fwd_2[1], groups, -1)

    back_sum = sum_three(after(back_0[0], *fwd_2), back_left, back_right)
    fwd_to_left = add_half(fwd_1[1], fwd_top, 0)
    fwd_to_right = add_half(fwd_1[0], fwd_bottom, 1)
    return_bwd = send(after(back_sum, sent_rows, fwd_to_left, fwd_to_right))
    grad_w_in = exchanged_grad(
        sent_rows.reshape(rows_bwd.shape), [*pre_grad_0, *pre_grad_1, *pre_grad_2], 256
    )

    fwd_left = turned(fwd_to_left, groups, 1)
    fwd_right = turned(fwd_to_right, groups, -1)
    fwd_sum = sum_three(fwd_0[0], after(fwd_left, grad_w_in), fwd_right)
    return_fwd = send(after(fwd_sum, return_bwd))

    section_out = call(
        functools.partial(forward_out_kernel, cap_rows),
        token_shape,
        [arrival, gate_fwd[0], route_fwd[0], return_fwd],
        2 * pick_flops,
    )[0]
    input_grad = call(
        functools.partial(backward_out_kernel, cap_rows),
        token_shape,
        [saved_input[0], gain, cotangent, route_bwd[0], slot_bwd[0], return_bwd],
        pick_flops,
    )[0]
    return (section_out[None], input_grad[None], grad_w_in[None], grad_w_out[None])


def solution(mesh):
    placed = (
        P("section", "expert", None),
        P("section", "expert", None),
        P("section", "expert", None),
        P("section", None),
        P("section", "expert", None),
        P("section", "expert", None),
        P("section", "expert", None),
        P("section", "expert", None),
        P("section", "expert", None),
        P("section", None, "expert"),
        P("section", "expert", None),
        P("section", "expert", None),
    )
    return jax.shard_map(
        body,
        mesh=mesh,
        in_specs=placed,
        out_specs=(
            P("section", "expert", None),
            P("section", "expert", None),
            P("section", None, "expert"),
            P("section", "expert", None),
        ),
        check_vma=False,
    )
```
